32 devices in a mesh: region: 2 (over core), tile: 16 (over z, y, x).
Axes of the slice: x: 2, y: 2, z: 4, core: 2. Of those that a mesh axis runs over, the one named last changes fastest.
Arguments:
- ens_obs: bfloat16 [4096, 512], P(('region', 'tile')), may hold values from -6 to 6
- obs_values: float32 [4096], P(('region', 'tile')), may hold values from -8 to 8
- obs_var: float32 [4096], P(('region', 'tile')), may hold values from 0.25 to 4
- edge_up: int32 [1024], P(('region', 'tile')), may hold values from 0 to 127
- edge_down: int32 [1024], P(('region', 'tile')), may hold values from 0 to 127
- loc_local: float32 [64, 2048], P(('region', 'tile')), may hold values from 0.02 to 1
- loc_edge: float32 [64, 1024], P(('region', 'tile')), may hold values from 0.02 to 1
- states: bfloat16 [2, 8192, 512], P(None, ('region', 'tile')), may hold values from -6 to 6
- box_ids: int32 [8192], P(('region', 'tile')), may hold values from 0 to 1
Outputs:
- analysis: bfloat16 [2, 8192, 512], P(None, ('region', 'tile'))
The draws below stay inside these ranges and needn't reach their ends.
All inputs are finite; a program needn't handle non-finite values.
Results may differ from the reference program's by a relative error of at most 0.0095.
Values may be sent and summed in bfloat16 or wider, within the bound.
A program may use at most 128 MiB of HBM per device.

```python
import math
import jax
import jax.numpy as jnp
from jax import lax

K = 512
OBS_DEV = 128
EDGE = 32
BOX_DEV = 2
CELLS_DEV = 256
FIELDS = 2
NOBS = 4096
NCELL = 8192
NBOX = 64
LOCAL_POOL = 2048
EDGE_POOL = 1024
N_REGION = 2
N_TILE = 16


def with_ends(entries, rng, smallest, top_value):
    dims = entries.shape
    place = [jax.random.randint(jax.random.fold_in(rng, axis), (), 0, dims[axis]) for axis in range(len(dims))]
    entries = entries.at[tuple(place)].set(smallest)
    longest = dims.index(max(dims))
    place[longest] = (place[longest] + 1) % dims[longest]
    return entries.at[tuple(place)].set(top_value)


def steps_of(stream_key, shape, pieces, low, largest):
    factor_of, own = 1.0, jax.random.fold_in(stream_key, 6)
    for axis_at, shards_of in pieces:
        heights = jnp.exp(jax.random.uniform(jax.random.fold_in(own, axis_at), (shards_of,), jnp.float32, low / len(pieces), largest / len(pieces)))
        factor_of = factor_of * jnp.repeat(heights, shape[axis_at] // shards_of).reshape([-1 if axis == axis_at else 1 for axis in range(len(shape))])
    return factor_of


def gaussian(stream_key, shape, deviation, limit, cuts=(), kind=jnp.bfloat16):
    drawn = jax.random.normal(stream_key, shape, jnp.float32) * deviation
    if len(cuts) > 0:
        drawn = steps_of(stream_key, shape, cuts, -0.22, 0.18) * drawn
    return jnp.clip(drawn, min=-limit, max=limit).astype(kind)


def setup_inputs(seed: int = 0) -> dict:
    arg_keys = jax.random.split(jax.random.key(seed), 10)
    ens_obs = gaussian(arg_keys[0], (NOBS, K), 1.0, 6.0, ((0, 32),))
    obs_values = gaussian(arg_keys[1], (NOBS,), 1.5, 8.0, ((0, 32),), jnp.float32)
    obs_var = jnp.clip(jnp.exp(math.log(4.0) - 2.7725887 * jax.random.uniform(arg_keys[2], (NOBS,), jnp.float32) ** steps_of(arg_keys[2], (NOBS,), ((0, 32),), -0.2, 0.2)), 0.25, 4.0)
    edge_up = with_ends(jax.random.randint(arg_keys[3], (N_REGION * N_TILE * EDGE,), 0, OBS_DEV), jax.random.fold_in(arg_keys[3], 1), 0, OBS_DEV - 1).astype(jnp.int32)
    edge_down = with_ends(jax.random.randint(arg_keys[4], (N_REGION * N_TILE * EDGE,), 0, OBS_DEV), jax.random.fold_in(arg_keys[4], 1), 0, OBS_DEV - 1).astype(jnp.int32)
    loc_local = jnp.clip(jnp.exp(math.log(1.0) - 3.912023 * jax.random.uniform(arg_keys[5], (NBOX, LOCAL_POOL), jnp.float32) ** steps_of(arg_keys[5], (NBOX, LOCAL_POOL), ((0, 32),), -0.2, 0.2)), 0.02, 1.0)
    loc_edge = jnp.clip(jnp.exp(math.log(1.0) - 3.912023 * jax.random.uniform(arg_keys[6], (NBOX, EDGE_POOL), jnp.float32) ** steps_of(arg_keys[6], (NBOX, EDGE_POOL), ((0, 32),), -0.2, 0.2)), 0.02, 1.0)
    states = gaussian(arg_keys[7], (FIELDS, NCELL, K), 1.0, 6.0, ((1, 32),))
    box_ids = with_ends(jax.random.randint(arg_keys[8], (NCELL,), 0, BOX_DEV), jax.random.fold_in(arg_keys[8], 1), 0, BOX_DEV - 1).astype(jnp.int32)
    return dict(ens_obs=ens_obs, obs_values=obs_values, obs_var=obs_var, edge_up=edge_up, edge_down=edge_down, loc_local=loc_local, loc_edge=loc_edge, states=states, box_ids=box_ids)


def obs_terms(anomaly, obs_info, weights):
    anom_wide = anomaly.astype(jnp.float32)
    obs_scale = weights * obs_info[:, 0].astype(jnp.float32)[None, :]
    scaled = (anom_wide[None] * obs_scale[:, :, None]).astype(jnp.bfloat16)
    scaled = lax.optimization_barrier(scaled).astype(jnp.float32)
    gram_sum = jnp.einsum('bpi,pj->bij', scaled, anom_wide, precision=lax.Precision.HIGHEST)
    weighted = (obs_scale * obs_info[:, 1].astype(jnp.float32)[None, :]).astype(jnp.bfloat16)
    weighted = lax.optimization_barrier(weighted).astype(jnp.float32)
    innov_sum = jnp.einsum('bp,pj->bj', weighted, anom_wide, precision=lax.Precision.HIGHEST)
    return (gram_sum, innov_sum)

def make_transform(gram_sum, innov_sum):
    members = gram_sum.shape[-1]
    identity = jnp.eye(members, dtype=jnp.float32)
    system = gram_sum + (members - 1.0) * identity
    right_sides = jnp.concatenate([jnp.broadcast_to(identity, system.shape), innov_sum[:, :, None]], axis=2)
    solved = jnp.linalg.solve(system, right_sides)
    inverse = solved[:, :, :members]
    wbar = solved[:, :, members]
    transform = 0.5 * identity + 0.5 * (members - 1.0) * inverse + wbar[:, :, None]
    return transform.astype(jnp.bfloat16)

def update_cells(states_dev, boxes_dev, transform):
    wide = states_dev.astype(jnp.float32)
    smean = jnp.mean(wide, axis=2)
    state_anomaly = (wide - smean[:, :, None]).astype(jnp.bfloat16)
    state_anomaly = lax.optimization_barrier(state_anomaly).astype(jnp.float32)
    updates = jnp.einsum('fck,bkj->bfcj', state_anomaly, transform.astype(jnp.float32), precision=lax.Precision.HIGHEST)
    box_range = jnp.arange(transform.shape[0], dtype=jnp.int32)
    selector = (boxes_dev[None, :] == box_range[:, None]).astype(jnp.float32)
    total = jnp.sum(selector[:, None, :, None] * updates, axis=0)
    return (smean[:, :, None] + total).astype(jnp.bfloat16)

def reference(ens_obs, obs_values, obs_var, edge_up, edge_down, loc_local, loc_edge, states, box_ids):
    regions = N_REGION
    tile_count = N_TILE
    wide = ens_obs.astype(jnp.float32).reshape(regions, tile_count, OBS_DEV, K)
    ymean = jnp.mean(wide, axis=3)
    anomaly = (wide - ymean[..., None]).astype(jnp.bfloat16)
    inv_var = 1.0 / obs_var.reshape(regions, tile_count, OBS_DEV)
    innov = obs_values.reshape(regions, tile_count, OBS_DEV) - ymean
    obs_info = jnp.stack([inv_var, innov], axis=-1).astype(jnp.bfloat16)
    up_index = edge_up.reshape(regions, tile_count, EDGE).astype(jnp.int32)
    down_index = edge_down.reshape(regions, tile_count, EDGE).astype(jnp.int32)
    sent_up_a = jnp.take_along_axis(anomaly, up_index[..., None], axis=2)
    sent_up_i = jnp.take_along_axis(obs_info, up_index[..., None], axis=2)
    sent_down_a = jnp.take_along_axis(anomaly, down_index[..., None], axis=2)
    sent_down_i = jnp.take_along_axis(obs_info, down_index[..., None], axis=2)
    lower_a = jnp.concatenate([jnp.zeros_like(sent_up_a[:1]), sent_up_a[:-1]], axis=0)
    lower_i = jnp.concatenate([jnp.zeros_like(sent_up_i[:1]), sent_up_i[:-1]], axis=0)
    upper_a = jnp.concatenate([sent_down_a[1:], jnp.zeros_like(sent_down_a[:1])], axis=0)
    upper_i = jnp.concatenate([sent_down_i[1:], jnp.zeros_like(sent_down_i[:1])], axis=0)
    edge_a = jnp.concatenate([lower_a, upper_a], axis=2)
    edge_i = jnp.concatenate([lower_i, upper_i], axis=2)
    local_w = loc_local.reshape(regions, tile_count, BOX_DEV, LOCAL_POOL)
    edge_w = loc_edge.reshape(regions, tile_count, BOX_DEV, EDGE_POOL)
    states_dev = jnp.transpose(states.reshape(FIELDS, regions, tile_count, CELLS_DEV, K), (1, 2, 0, 3, 4))
    boxes = box_ids.reshape(regions, tile_count, CELLS_DEV).astype(jnp.int32)

    def one_device(index):
        region_at = index // tile_count
        tile_at = index % tile_count
        pool_a = anomaly[region_at].reshape(LOCAL_POOL, K)
        pool_i = obs_info[region_at].reshape(LOCAL_POOL, 2)
        gram_one, innov_one = obs_terms(pool_a, pool_i, local_w[region_at, tile_at])
        rim_a = edge_a[region_at].reshape(EDGE_POOL, K)
        rim_i = edge_i[region_at].reshape(EDGE_POOL, 2)
        gram_two, innov_two = obs_terms(rim_a, rim_i, edge_w[region_at, tile_at])
        transform = make_transform(gram_one + gram_two, innov_one + innov_two)
        return update_cells(states_dev[region_at, tile_at], boxes[region_at, tile_at], transform)
    result = lax.map(one_device, jnp.arange(regions * tile_count, dtype=jnp.int32))
    result = result.reshape(regions, tile_count, FIELDS, CELLS_DEV, K)
    return jnp.transpose(result, (2, 0, 1, 3, 4)).reshape(FIELDS, NCELL, K)
```

```python
import jax
import jax.numpy as jnp
from jax import lax
from jax.experimental import pallas as pl
from jax.experimental.pallas import tpu as pltpu
from jax.sharding import PartitionSpec as P


def passed_along(block, axis, distance):
    devices = range(lax.axis_size(axis))
    route = [(i - distance, i) for i in devices if i - distance in devices]
    return lax.ppermute(block, axis, route)


def obs_terms(anomaly, obs_info, weights):
    obs_scale = weights * obs_info[:, 0].astype(jnp.float32)[None, :]
    scaled = (anomaly[None] * obs_scale[:, :, None]).astype(jnp.bfloat16)
    gram_sum = jnp.einsum("bpi,pj->bij", scaled, anomaly, preferred_element_type=jnp.float32)
    weighted = (obs_scale * obs_info[:, 1].astype(jnp.float32)[None, :]).astype(jnp.bfloat16)
    innov_sum = jnp.einsum("bp,pj->bj", weighted, anomaly, preferred_element_type=jnp.float32)
    return (gram_sum, innov_sum)


def split(x):
    high = x.astype(jnp.bfloat16)
    return high, (x - high.astype(jnp.float32)).astype(jnp.bfloat16)


def dot_once(left, right):
    return jnp.dot(left.astype(jnp.bfloat16), right.astype(jnp.bfloat16), preferred_element_type=jnp.float32)


def dot_thrice(left, right):
    left_high, left_low = split(left)
    right_high, right_low = split(right)
    mixed = jnp.dot(left_low, right_high, preferred_element_type=jnp.float32)
    mixed += jnp.dot(left_high, right_low, preferred_element_type=jnp.float32)
    return mixed + jnp.dot(left_high, right_high, preferred_element_type=jnp.float32)


def dot_full(left, right):
    return jnp.dot(left, right, precision=lax.Precision.HIGHEST, preferred_element_type=jnp.float32)


def shrink(error):
    return error * error / (2.0 - error * error)


def analyse_kernel(gram_ref, innov_ref, states_ref, ids_ref, out_ref, system, guess):
    boxes, members, _ = gram_ref.shape
    fields, cells, _ = states_ref.shape
    rows = lax.broadcasted_iota(jnp.int32, (members, members), 0)
    columns = lax.broadcasted_iota(jnp.int32, (members, members), 1)
    identity = (rows == columns).astype(jnp.float32)
    ridge = members - 1.0

    worst = jnp.float32(0.0)
    errors = []
    for b in range(boxes):
        full = gram_ref[b] + ridge * identity
        top = jnp.maximum(jnp.max(jnp.sum(jnp.abs(full), axis=0, keepdims=True)), ridge)
        first = 2.0 / (top + ridge)
        error = (top - ridge) / (top + ridge)
        mu = 2.0 / (2.0 - error * error)
        system[b] = full
        guess[b] = (mu * first) * (2.0 * identity - first * full)
        errors.append(shrink(error))
        worst = jnp.maximum(worst, top / ridge)

    def refine(dot):
        def step(carried):
            after = []
            for b in range(boxes):
                error = carried[b]
                mu = 2.0 / (2.0 - error * error)
                left = 2.0 * identity - dot(system[b], guess[b])
                guess[b] = mu * dot(guess[b], left)
                after.append(shrink(error))
            return tuple(after)
        return step

    def above(limit, allowed):
        def proceed(carried):
            top = carried[0]
            for error in carried[1:]:
                top = jnp.maximum(top, error)
            return jnp.logical_and(allowed, top > limit)
        return proceed

    easy = worst < 64.0
    hard = worst > 2048.0
    errors = lax.while_loop(above(0.005, easy), refine(dot_once), tuple(errors))
    errors = tuple(jnp.maximum(error, 0.02) for error in errors)
    errors = lax.while_loop(above(3e-4, jnp.logical_not(hard)), refine(dot_thrice), errors)
    errors = lax.while_loop(above(1e-6, hard), refine(dot_full), errors)

    wide = states_ref[...].astype(jnp.float32).reshape(fields * cells, members)
    smean = jnp.sum(wide, axis=1, keepdims=True) * (1.0 / members)
    anomaly = (wide - smean).astype(jnp.bfloat16)
    here = lax.broadcasted_iota(jnp.int32, (cells, cells), 0) == lax.broadcasted_iota(jnp.int32, (cells, cells), 1)
    spread = jnp.broadcast_to(ids_ref[...].astype(jnp.float32), (cells, cells))
    ids = jnp.sum(jnp.where(here, spread, 0.0), axis=1, keepdims=True)
    ids = jnp.concatenate([ids] * fields, axis=0)
    total = jnp.zeros((fields * cells, members), jnp.float32)
    for b in range(boxes):
        inverse = guess[b]
        wbar = jnp.sum(inverse * innov_ref[b:b + 1, :], axis=1, keepdims=True)
        transform = (0.5 * identity + (0.5 * ridge) * inverse + wbar).astype(jnp.bfloat16)
        update = jnp.dot(anomaly, transform, preferred_element_type=jnp.float32)
        total = jnp.where(ids == float(b), update, total)
    out_ref[...] = (smean + total).astype(jnp.bfloat16).reshape(fields, cells, members)


def analyse(gram, innov, states, box_ids):
    boxes, members, _ = gram.shape
    return pl.pallas_call(
        analyse_kernel,
        out_shape=jax.ShapeDtypeStruct(states.shape, jnp.bfloat16),
        in_specs=[pl.BlockSpec(memory_space=pltpu.VMEM)] * 4,
        out_specs=pl.BlockSpec(memory_space=pltpu.VMEM),
        scratch_shapes=[
            pltpu.VMEM((boxes, members, members), jnp.float32),
            pltpu.VMEM((boxes, members, members), jnp.float32),
        ],
        compiler_params=pltpu.CompilerParams(vmem_limit_bytes=48 * 1024 * 1024),
        name="analyse",
    )(gram, innov, states, box_ids.reshape(1, -1))


def body(ens_obs, obs_values, obs_var, edge_up, edge_down, loc_local, loc_edge, states, box_ids):
    record_count = ens_obs.shape[0]
    members = ens_obs.shape[1]
    ymean = jnp.mean(ens_obs, axis=1, dtype=jnp.float32)
    anomaly = (ens_obs.astype(jnp.float32) - ymean[:, None]).astype(jnp.bfloat16)
    obs_info = jnp.stack([1.0 / obs_var, obs_values - ymean], axis=1).astype(jnp.bfloat16)
    lower_a, lower_i = passed_along((anomaly[edge_up], obs_info[edge_up]), "region", 1)
    upper_a, upper_i = passed_along((anomaly[edge_down], obs_info[edge_down]), "region", -1)
    edge_anom = jnp.concatenate([lower_a, upper_a], axis=0)
    edge_info = jnp.concatenate([lower_i, upper_i], axis=0)
    block_anom = jnp.concatenate([anomaly, edge_anom], axis=0)
    block_info = jnp.concatenate([obs_info, edge_info], axis=0)
    all_anom, all_info = (
        lax.all_gather(block_anom, "tile", axis=0, tiled=True),
        lax.all_gather(block_info, "tile", axis=0, tiled=True),
    )
    tile_count = lax.axis_size("tile")
    pool_rows = block_anom.shape[0]
    all_anom = all_anom.reshape(tile_count, pool_rows, members)
    all_info = all_info.reshape(tile_count, pool_rows, 2)
    gram_one, innov_one = obs_terms(
        all_anom[:, :record_count].reshape(-1, members),
        all_info[:, :record_count].reshape(-1, 2),
        loc_local,
    )
    gram_two, innov_two = obs_terms(
        all_anom[:, record_count:].reshape(-1, members),
        all_info[:, record_count:].reshape(-1, 2),
        loc_edge,
    )
    return analyse(gram_one + gram_two, innov_one + innov_two, states, box_ids)


def solution(mesh):
    return jax.shard_map(
        body,
        mesh=mesh,
        in_specs=(
            P(("region", "tile"), None),
            P(("region", "tile")),
            P(("region", "tile")),
            P(("region", "tile")),
            P(("region", "tile")),
            P(("region", "tile"), None),
            P(("region", "tile"), None),
            P(None, ("region", "tile"), None),
            P(("region", "tile")),
        ),
        out_specs=P(None, ("region", "tile"), None),
        check_vma=False,
    )
```

```python
import functools
import jax
import jax.numpy as jnp
from jax import lax
from jax.experimental import pallas as pl
from jax.experimental.pallas import tpu as pltpu
from jax.sharding import PartitionSpec as P


INFO_ROWS = 16


def tile_sides(tiles):
    return 4, 2, tiles // 8


def gather_kernel(regions, tiles, ens_ref, values_ref, var_ref, up_ref, down_ref, local_ref, edge_ref,
                  gram_ref, innov_ref, pool, weights, leaving, arriving,
                  send_sem, recv_sem, edge_send_sem, edge_recv_sem):
    region = lax.axis_index("region")
    tile = lax.axis_index("tile")
    z_side, y_side, x_side = tile_sides(tiles)
    plane = y_side * x_side
    at_z, at_y, at_x = tile // plane, (tile // x_side) % y_side, tile % x_side
    at = tile % plane
    records, members = ens_ref.shape
    boxes = local_ref.shape[0]
    edges = up_ref.shape[1]
    sides = leaving.shape[0]
    rows = records + sides * edges
    block_rows = pool.shape[2]
    cut = (block_rows // 2 + 15) // 16 * 16

    x_others = [at_y * x_side + (at_x + d) % x_side for d in range(1, x_side)]
    y_others = [(at_y + d) % y_side * x_side + at_x for d in range(1, y_side)]
    z_others = [(at_z + d) % z_side for d in range(1, z_side)]
    if sides == 1:
        partners = [(1 - region, 0)]
    else:
        partners = [((region + 1) % regions, 0), ((region + regions - 1) % regions, 1)]

    barrier = pltpu.get_barrier_semaphore()
    greeted = [(region, z * plane + at) for z in z_others]
    greeted += [(region, at_z * plane + p) for p in x_others + y_others]
    greeted += [(partner, tile) for partner, _ in partners]
    for device in greeted:
        pl.semaphore_signal(barrier, inc=1, device_id=device, device_id_type=pl.DeviceIdType.MESH)

    wide = ens_ref[...].astype(jnp.float32)
    ymean = jnp.sum(wide, axis=1, keepdims=True) * (1.0 / members)
    anomaly = (wide - ymean).astype(jnp.bfloat16)
    row_at = lax.broadcasted_iota(jnp.int32, (records, records), 0)
    column_at = lax.broadcasted_iota(jnp.int32, (records, records), 1)
    ymean_row = jnp.sum(jnp.where(row_at == column_at, ymean, 0.0), axis=0, keepdims=True)
    info = jnp.concatenate(
        [1.0 / var_ref[...], values_ref[...] - ymean_row, jnp.zeros((INFO_ROWS - 2, records), jnp.float32)], axis=0
    ).astype(jnp.bfloat16)

    def picked(index_row, keep):
        index = jnp.concatenate([index_row] * (records // edges), axis=1)
        chosen = jnp.where(row_at == index, keep, 0.0)
        far_info = jnp.dot(info, chosen.astype(jnp.bfloat16), preferred_element_type=jnp.float32)
        chosen = chosen.T[:edges].astype(jnp.bfloat16)
        far = jnp.dot(chosen, anomaly, preferred_element_type=jnp.float32)
        return far.astype(jnp.bfloat16), far_info.astype(jnp.bfloat16)

    if sides == 1:
        chosen_row = jnp.where(region == 0, up_ref[...], down_ref[...])
        going = [picked(chosen_row, 1.0)]
    else:
        going = [
            picked(up_ref[...], jnp.where(region == regions - 1, 0.0, 1.0)),
            picked(down_ref[...], jnp.where(region == 0, 0.0, 1.0)),
        ]
    for side, (far, far_info) in enumerate(going):
        leaving[side, :edges, :] = far
        leaving[side, edges:, :records] = far_info
        leaving[side, edges:, records:] = jnp.zeros((INFO_ROWS, members - records), jnp.bfloat16)
    pool[at, at_z, :records, :] = anomaly

    pl.semaphore_wait(barrier, len(greeted))
    started = []
    crossing = []
    for partner, side in partners:
        copy = pltpu.make_async_remote_copy(
            src_ref=leaving.at[side], dst_ref=arriving.at[side],
            send_sem=edge_send_sem.at[side], recv_sem=edge_recv_sem.at[side],
            device_id=(partner, tile), device_id_type=pl.DeviceIdType.MESH,
        )
        copy.start()
        crossing.append(copy)
    for copy in crossing:
        copy.wait_recv()
    pieces = [info]
    for side in range(sides):
        pool[at, at_z, pl.ds(records + side * edges, edges), :] = arriving[side, :edges, :]
        pieces.append(arriving[side, edges:, :edges])
    pieces.append(jnp.zeros((INFO_ROWS, members - rows), jnp.bfloat16))
    pool[at, at_z, rows:, :] = jnp.concatenate(pieces, axis=1)

    def piece(place, z, part):
        if part is None:
            return pool.at[place, z]
        if part == 0:
            return pool.at[place, z, pl.ds(0, cut)]
        return pool.at[place, z, pl.ds(cut, block_rows - cut)]

    def describe(place, z, part, device, number):
        return pltpu.make_async_remote_copy(
            src_ref=piece(place, z, part), dst_ref=piece(place, z, part),
            send_sem=send_sem.at[number], recv_sem=recv_sem.at[1 if part == 1 else 0, place, z],
            device_id=device, device_id_type=pl.DeviceIdType.MESH,
        )

    def send(place, z, part, device):
        copy = describe(place, z, part, device, len(started))
        copy.start()
        started.append(copy)

    def await_piece(place, z, part=None):
        describe(place, z, part, (region, tile), 0).wait_recv()

    def spread(z):
        for p in x_others + y_others:
            send(at, z, None, (region, at_z * plane + p))

    for z in z_others:
        send(at, at_z, None, (region, z * plane + at))
    spread(at_z)

    edge_columns = 2 * edges
    for t in range(tiles):
        weights[t, :, :records] = local_ref[:, t * records:(t + 1) * records]
        near = edge_ref[:, t * edge_columns:(t + 1) * edge_columns]
        if sides == 1:
            near = jnp.where(region == 0, near[:, edges:], near[:, :edges])
        weights[t, :, records:rows] = near

    def absorb(place, first=False):
        block = pool[place]
        data = jnp.concatenate(
            [block[:, :records].reshape(z_side * records, members),
             block[:, records:rows].reshape(z_side * (rows - records), members)], axis=0)
        turned = data.astype(jnp.float32).T
        inverse_var = [block[z, rows:, :rows].astype(jnp.float32)[0:1] for z in range(z_side)]
        innovation = [block[z, rows:, :rows].astype(jnp.float32)[1:2] for z in range(z_side)]
        loc = [weights[z * plane + place][:, :rows] for z in range(z_side)]

        def ordered(parts):
            return jnp.concatenate([p[:, :records] for p in parts] + [p[:, records:] for p in parts], axis=1)

        scale = ordered(loc) * ordered(inverse_var)
        weighted = (scale * ordered(innovation)).astype(jnp.bfloat16)
        more = jnp.dot(weighted, data, preferred_element_type=jnp.float32)
        innov_ref[...] = more if first else innov_ref[...] + more
        for b in range(boxes):
            scaled = (turned * scale[b:b + 1]).astype(jnp.bfloat16)
            more = jnp.dot(scaled, data, preferred_element_type=jnp.float32)
            gram_ref[b] = more if first else gram_ref[b] + more

    order = [(at_z + z_side - d) % z_side for d in range(1, z_side)]
    for z in order:
        await_piece(at, z)
        spread(z)
    absorb(at, first=True)
    for z in [at_z] + order:
        for p in x_others:
            await_piece(p, z)
            for d in range(1, y_side):
                far = (at_y + d) % y_side * x_side + at_x
                send(p, z, 0, (region, at_z * plane + far))
        for p in y_others:
            await_piece(p, z)
            for d in range(1, x_side):
                far = at_y * x_side + (at_x + d) % x_side
                send(p, z, 1, (region, at_z * plane + far))
    for p in x_others + y_others:
        absorb(p)
    for dy in range(1, y_side):
        for dx in range(1, x_side):
            far = (at_y + dy) % y_side * x_side + (at_x + dx) % x_side
            for z in range(z_side):
                await_piece(far, z, 0)
                await_piece(far, z, 1)
            absorb(far)
    for copy in crossing + started:
        copy.wait_send()


def gathered_sums(ens_obs, obs_values, obs_var, edge_up, edge_down, loc_local, loc_edge):
    regions, tiles = lax.axis_size("region"), lax.axis_size("tile")
    records, members = ens_obs.shape
    boxes, edges = loc_local.shape[0], edge_up.shape[0]
    sides = 1 if regions == 2 else 2
    rows = records + sides * edges
    block_rows = rows + INFO_ROWS
    z_side, y_side, x_side = tile_sides(tiles)
    plane = y_side * x_side
    sends = z_side - 1 + z_side * (x_side + y_side - 2) + 2 * z_side * (x_side - 1) * (y_side - 1)
    return pl.pallas_call(
        functools.partial(gather_kernel, regions, tiles),
        out_shape=(
            jax.ShapeDtypeStruct((boxes, members, members), jnp.float32),
            jax.ShapeDtypeStruct((boxes, members), jnp.float32),
        ),
        in_specs=[pl.BlockSpec(memory_space=pltpu.VMEM)] * 7,
        out_specs=[pl.BlockSpec(memory_space=pltpu.VMEM)] * 2,
        scratch_shapes=[
            pltpu.VMEM((plane, z_side, block_rows, members), jnp.bfloat16),
            pltpu.VMEM((tiles, boxes, (rows + 127) // 128 * 128), jnp.float32),
            pltpu.VMEM((sides, edges + INFO_ROWS, members), jnp.bfloat16),
            pltpu.VMEM((sides, edges + INFO_ROWS, members), jnp.bfloat16),
            pltpu.SemaphoreType.DMA((sends,)),
            pltpu.SemaphoreType.DMA((2, plane, z_side)),
            pltpu.SemaphoreType.DMA((sides,)),
            pltpu.SemaphoreType.DMA((sides,)),
        ],
        compiler_params=pltpu.CompilerParams(
            collective_id=0, has_side_effects=True, vmem_limit_bytes=48 * 1024 * 1024
        ),
        name="gather_gram",
    )(ens_obs, obs_values.reshape(1, -1), obs_var.reshape(1, -1), edge_up.reshape(1, -1),
      edge_down.reshape(1, -1), loc_local, loc_edge)


def split(x):
    high = x.astype(jnp.bfloat16)
    return high, (x - high.astype(jnp.float32)).astype(jnp.bfloat16)


def dot_once(left, right):
    return jnp.dot(left.astype(jnp.bfloat16), right.astype(jnp.bfloat16), preferred_element_type=jnp.float32)


def dot_thrice(left, right):
    left_high, left_low = split(left)
    right_high, right_low = split(right)
    mixed = jnp.dot(left_low, right_high, preferred_element_type=jnp.float32)
    mixed += jnp.dot(left_high, right_low, preferred_element_type=jnp.float32)
    return mixed + jnp.dot(left_high, right_high, preferred_element_type=jnp.float32)


def dot_full(left, right):
    return jnp.dot(left, right, precision=lax.Precision.HIGHEST, preferred_element_type=jnp.float32)


def shrink(error):
    return error * error / (2.0 - error * error)


def analyse_kernel(gram_ref, innov_ref, states_ref, ids_ref, out_ref, system, guess):
    boxes, members, _ = gram_ref.shape
    fields, cells, _ = states_ref.shape
    rows = lax.broadcasted_iota(jnp.int32, (members, members), 0)
    columns = lax.broadcasted_iota(jnp.int32, (members, members), 1)
    identity = (rows == columns).astype(jnp.float32)
    ridge = members - 1.0

    worst = jnp.float32(0.0)
    errors = []
    for b in range(boxes):
        full = gram_ref[b] + ridge * identity
        top = jnp.maximum(jnp.max(jnp.sum(jnp.abs(full), axis=0, keepdims=True)), ridge)
        first = 2.0 / (top + ridge)
        error = (top - ridge) / (top + ridge)
        mu = 2.0 / (2.0 - error * error)
        system[b] = full
        guess[b] = (mu * first) * (2.0 * identity - first * full)
        errors.append(shrink(error))
        worst = jnp.maximum(worst, top / ridge)

    def refine(dot):
        def step(carried):
            after = []
            for b in range(boxes):
                error = carried[b]
                mu = 2.0 / (2.0 - error * error)
                left = 2.0 * identity - dot(system[b], guess[b])
                guess[b] = mu * dot(guess[b], left)
                after.append(shrink(error))
            return tuple(after)
        return step

    def above(limit, allowed):
        def proceed(carried):
            top = carried[0]
            for error in carried[1:]:
                top = jnp.maximum(top, error)
            return jnp.logical_and(allowed, top > limit)
        return proceed

    easy = worst < 64.0
    hard = worst > 2048.0
    errors = lax.while_loop(above(0.005, easy), refine(dot_once), tuple(errors))
    errors = tuple(jnp.maximum(error, 0.02) for error in errors)
    errors = lax.while_loop(above(3e-4, jnp.logical_not(hard)), refine(dot_thrice), errors)
    errors = lax.while_loop(above(1e-6, hard), refine(dot_full), errors)

    wide = states_ref[...].astype(jnp.float32).reshape(fields * cells, members)
    smean = jnp.sum(wide, axis=1, keepdims=True) * (1.0 / members)
    anomaly = (wide - smean).astype(jnp.bfloat16)
    here = lax.broadcasted_iota(jnp.int32, (cells, cells), 0) == lax.broadcasted_iota(jnp.int32, (cells, cells), 1)
    spread = jnp.broadcast_to(ids_ref[...].astype(jnp.float32), (cells, cells))
    ids = jnp.sum(jnp.where(here, spread, 0.0), axis=1, keepdims=True)
    ids = jnp.concatenate([ids] * fields, axis=0)
    total = jnp.zeros((fields * cells, members), jnp.float32)
    for b in range(boxes):
        inverse = guess[b]
        wbar = jnp.sum(inverse * innov_ref[b:b + 1, :], axis=1, keepdims=True)
        transform = (0.5 * identity + (0.5 * ridge) * inverse + wbar).astype(jnp.bfloat16)
        update = jnp.dot(anomaly, transform, preferred_element_type=jnp.float32)
        total = jnp.where(ids == float(b), update, total)
    out_ref[...] = (smean + total).astype(jnp.bfloat16).reshape(fields, cells, members)


def analyse(gram, innov, states, box_ids):
    boxes, members, _ = gram.shape
    return pl.pallas_call(
        analyse_kernel,
        out_shape=jax.ShapeDtypeStruct(states.shape, jnp.bfloat16),
        in_specs=[pl.BlockSpec(memory_space=pltpu.VMEM)] * 4,
        out_specs=pl.BlockSpec(memory_space=pltpu.VMEM),
        scratch_shapes=[
            pltpu.VMEM((boxes, members, members), jnp.float32),
            pltpu.VMEM((boxes, members, members), jnp.float32),
        ],
        compiler_params=pltpu.CompilerParams(vmem_limit_bytes=48 * 1024 * 1024),
        name="analyse",
    )(gram, innov, states, box_ids.reshape(1, -1))


def body(ens_obs, obs_values, obs_var, edge_up, edge_down, loc_local, loc_edge, states, box_ids):
    gram, innov = gathered_sums(ens_obs, obs_values, obs_var, edge_up, edge_down, loc_local, loc_edge)
    return analyse(gram, innov, states, box_ids)


def solution(mesh):
    return jax.shard_map(
        body,
        mesh=mesh,
        in_specs=(
            P(("region", "tile"), None),
            P(("region", "tile")),
            P(("region", "tile")),
            P(("region", "tile")),
            P(("region", "tile")),
            P(("region", "tile"), None),
            P(("region", "tile"), None),
            P(None, ("region", "tile"), None),
            P(("region", "tile")),
        ),
        out_specs=P(None, ("region", "tile"), None),
        check_vma=False,
    )
```

```python
import functools
import jax
import jax.numpy as jnp
from jax import lax
from jax.experimental import pallas as pl
from jax.experimental.pallas import tpu as pltpu
from jax.sharding import PartitionSpec as P


INFO_ROWS = 16


def tile_sides(tiles):
    return 4, 2, tiles // 8


def gather_kernel(regions, tiles, ens_hbm, values_hbm, var_hbm, up_hbm, down_hbm, local_hbm, edge_hbm,
                  gram_ref, innov_ref, ens_ref, values_ref, var_ref, up_ref, down_ref, local_ref, edge_ref,
                  copy_sem, pool, weights, leaving, arriving,
                  send_sem, recv_sem, edge_send_sem, edge_recv_sem):
    region = lax.axis_index("region")
    tile = lax.axis_index("tile")
    fetched = []
    for number, (far, near) in enumerate([
        (ens_hbm, ens_ref), (values_hbm, values_ref), (var_hbm, var_ref), (up_hbm, up_ref),
        (down_hbm, down_ref), (local_hbm, local_ref), (edge_hbm, edge_ref),
    ]):
        fetched.append(pltpu.make_async_copy(far, near, copy_sem.at[number]))
        fetched[-1].start()
    z_side, y_side, x_side = tile_sides(tiles)
    plane = y_side * x_side
    at_z, at_y, at_x = tile // plane, (tile // x_side) % y_side, tile % x_side
    at = tile % plane
    records, members = ens_ref.shape
    boxes = local_ref.shape[0]
    edges = up_ref.shape[1]
    sides = leaving.shape[0]
    rows = records + sides * edges
    block_rows = pool.shape[2]
    cut = (block_rows // 2 + 15) // 16 * 16

    x_others = [at_y * x_side + (at_x + d) % x_side for d in range(1, x_side)]
    y_others = [(at_y + d) % y_side * x_side + at_x for d in range(1, y_side)]
    z_others = [(at_z + d) % z_side for d in range(1, z_side)]
    if sides == 1:
        partners = [(1 - region, 0)]
    else:
        partners = [((region + 1) % regions, 0), ((region + regions - 1) % regions, 1)]

    barrier = pltpu.get_barrier_semaphore()
    greeted = [(region, z * plane + at) for z in z_others]
    greeted += [(region, at_z * plane + p) for p in x_others + y_others]
    greeted += [(partner, tile) for partner, _ in partners]
    for device in greeted:
        pl.semaphore_signal(barrier, inc=1, device_id=device, device_id_type=pl.DeviceIdType.MESH)

    for copy in fetched[:5]:
        copy.wait()
    wide = ens_ref[...].astype(jnp.float32)
    ymean = jnp.sum(wide, axis=1, keepdims=True) * (1.0 / members)
    anomaly = (wide - ymean).astype(jnp.bfloat16)
    row_at = lax.broadcasted_iota(jnp.int32, (records, records), 0)
    column_at = lax.broadcasted_iota(jnp.int32, (records, records), 1)
    ymean_row = jnp.sum(jnp.where(row_at == column_at, ymean, 0.0), axis=0, keepdims=True)
    info = jnp.concatenate(
        [1.0 / var_ref[...], values_ref[...] - ymean_row, jnp.zeros((INFO_ROWS - 2, records), jnp.float32)], axis=0
    ).astype(jnp.bfloat16)

    def picked(index_row, keep):
        index = jnp.concatenate([index_row] * (records // edges), axis=1)
        chosen = jnp.where(row_at == index, keep, 0.0)
        far_info = jnp.dot(info, chosen.astype(jnp.bfloat16), preferred_element_type=jnp.float32)
        chosen = chosen.T[:edges].astype(jnp.bfloat16)
        far = jnp.dot(chosen, anomaly, preferred_element_type=jnp.float32)
        return far.astype(jnp.bfloat16), far_info.astype(jnp.bfloat16)

    if sides == 1:
        chosen_row = jnp.where(region == 0, up_ref[...], down_ref[...])
        going = [picked(chosen_row, 1.0)]
    else:
        going = [
            picked(up_ref[...], jnp.where(region == regions - 1, 0.0, 1.0)),
            picked(down_ref[...], jnp.where(region == 0, 0.0, 1.0)),
        ]
    for side, (far, far_info) in enumerate(going):
        leaving[side, :edges, :] = far
        leaving[side, edges:, :records] = far_info
        leaving[side, edges:, records:] = jnp.zeros((INFO_ROWS, members - records), jnp.bfloat16)
    pool[at, at_z, :records, :] = anomaly

    pl.semaphore_wait(barrier, len(greeted))
    started = []
    crossing = []
    for partner, side in partners:
        copy = pltpu.make_async_remote_copy(
            src_ref=leaving.at[side], dst_ref=arriving.at[side],
            send_sem=edge_send_sem.at[side], recv_sem=edge_recv_sem.at[side],
            device_id=(partner, tile), device_id_type=pl.DeviceIdType.MESH,
        )
        copy.start()
        crossing.append(copy)
    for copy in crossing:
        copy.wait_recv()
    pieces = [info]
    for side in range(sides):
        pool[at, at_z, pl.ds(records + side * edges, edges), :] = arriving[side, :edges, :]
        pieces.append(arriving[side, edges:, :edges])
    pieces.append(jnp.zeros((INFO_ROWS, members - rows), jnp.bfloat16))
    pool[at, at_z, rows:, :] = jnp.concatenate(pieces, axis=1)

    def piece(place, z, part):
        if part is None:
            return pool.at[place, z]
        if part == 0:
            return pool.at[place, z, pl.ds(0, cut)]
        return pool.at[place, z, pl.ds(cut, block_rows - cut)]

    def describe(place, z, part, device, number):
        return pltpu.make_async_remote_copy(
            src_ref=piece(place, z, part), dst_ref=piece(place, z, part),
            send_sem=send_sem.at[number], recv_sem=recv_sem.at[1 if part == 1 else 0, place, z],
            device_id=device, device_id_type=pl.DeviceIdType.MESH,
        )

    def send(place, z, part, device):
        copy = describe(place, z, part, device, len(started))
        copy.start()
        started.append(copy)

    def await_piece(place, z, part=None):
        describe(place, z, part, (region, tile), 0).wait_recv()

    def spread(z):
        for p in x_others + y_others:
            send(at, z, None, (region, at_z * plane + p))

    for z in z_others:
        send(at, at_z, None, (region, z * plane + at))
    spread(at_z)

    for copy in fetched[5:]:
        copy.wait()
    edge_columns = 2 * edges
    for t in range(tiles):
        weights[t, :, :records] = local_ref[:, t * records:(t + 1) * records]
        near = edge_ref[:, t * edge_columns:(t + 1) * edge_columns]
        if sides == 1:
            near = jnp.where(region == 0, near[:, edges:], near[:, :edges])
        weights[t, :, records:rows] = near

    def absorb(place, first=False):
        block = pool[place]
        data = jnp.concatenate(
            [block[:, :records].reshape(z_side * records, members),
             block[:, records:rows].reshape(z_side * (rows - records), members)], axis=0)
        turned = data.astype(jnp.float32).T
        inverse_var = [block[z, rows:, :rows].astype(jnp.float32)[0:1] for z in range(z_side)]
        innovation = [block[z, rows:, :rows].astype(jnp.float32)[1:2] for z in range(z_side)]
        loc = [weights[z * plane + place][:, :rows] for z in range(z_side)]

        def ordered(parts):
            return jnp.concatenate([p[:, :records] for p in parts] + [p[:, records:] for p in parts], axis=1)

        scale = ordered(loc) * ordered(inverse_var)
        weighted = (scale * ordered(innovation)).astype(jnp.bfloat16)
        more = jnp.dot(weighted, data, preferred_element_type=jnp.float32)
        innov_ref[...] = more if first else innov_ref[...] + more
        for b in range(boxes):
            scaled = (turned * scale[b:b + 1]).astype(jnp.bfloat16)
            more = jnp.dot(scaled, data, preferred_element_type=jnp.float32)
            gram_ref[b] = more if first else gram_ref[b] + more

    order = [(at_z + z_side - d) % z_side for d in range(1, z_side)]
    for z in order:
        await_piece(at, z)
        spread(z)
    absorb(at, first=True)
    for z in [at_z] + order:
        for p in x_others:
            await_piece(p, z)
            for d in range(1, y_side):
                far = (at_y + d) % y_side * x_side + at_x
                send(p, z, 0, (region, at_z * plane + far))
        for p in y_others:
            await_piece(p, z)
            for d in range(1, x_side):
                far = at_y * x_side + (at_x + d) % x_side
                send(p, z, 1, (region, at_z * plane + far))
    for p in x_others + y_others:
        absorb(p)
    for dy in range(1, y_side):
        for dx in range(1, x_side):
            far = (at_y + dy) % y_side * x_side + (at_x + dx) % x_side
            for z in range(z_side):
                await_piece(far, z, 0)
                await_piece(far, z, 1)
            absorb(far)
    for copy in crossing + started:
        copy.wait_send()


def gathered_sums(ens_obs, obs_values, obs_var, edge_up, edge_down, loc_local, loc_edge):
    regions, tiles = lax.axis_size("region"), lax.axis_size("tile")
    records, members = ens_obs.shape
    boxes, edges = loc_local.shape[0], edge_up.shape[0]
    sides = 1 if regions == 2 else 2
    rows = records + sides * edges
    block_rows = rows + INFO_ROWS
    z_side, y_side, x_side = tile_sides(tiles)
    plane = y_side * x_side
    sends = z_side - 1 + z_side * (x_side + y_side - 2) + 2 * z_side * (x_side - 1) * (y_side - 1)
    arrays = (ens_obs, obs_values.reshape(1, -1), obs_var.reshape(1, -1), edge_up.reshape(1, -1),
              edge_down.reshape(1, -1), loc_local, loc_edge)
    return pl.pallas_call(
        functools.partial(gather_kernel, regions, tiles),
        out_shape=(
            jax.ShapeDtypeStruct((boxes, members, members), jnp.float32),
            jax.ShapeDtypeStruct((boxes, members), jnp.float32),
        ),
        in_specs=[pl.BlockSpec(memory_space=pl.ANY)] * 7,
        out_specs=[pl.BlockSpec(memory_space=pltpu.VMEM)] * 2,
        scratch_shapes=[pltpu.VMEM(array.shape, array.dtype) for array in arrays] + [
            pltpu.SemaphoreType.DMA((len(arrays),)),
            pltpu.VMEM((plane, z_side, block_rows, members), jnp.bfloat16),
            pltpu.VMEM((tiles, boxes, (rows + 127) // 128 * 128), jnp.float32),
            pltpu.VMEM((sides, edges + INFO_ROWS, members), jnp.bfloat16),
            pltpu.VMEM((sides, edges + INFO_ROWS, members), jnp.bfloat16),
            pltpu.SemaphoreType.DMA((sends,)),
            pltpu.SemaphoreType.DMA((2, plane, z_side)),
            pltpu.SemaphoreType.DMA((sides,)),
            pltpu.SemaphoreType.DMA((sides,)),
        ],
        compiler_params=pltpu.CompilerParams(
            collective_id=0, has_side_effects=True, vmem_limit_bytes=56 * 1024 * 1024
        ),
        name="gather_gram",
    )(*arrays)


def split(x):
    high = x.astype(jnp.bfloat16)
    return high, (x - high.astype(jnp.float32)).astype(jnp.bfloat16)


def dot_thrice(left, right):
    left_high, left_low = split(left)
    right_high, right_low = split(right)
    mixed = jnp.dot(left_low, right_high, preferred_element_type=jnp.float32)
    mixed += jnp.dot(left_high, right_low, preferred_element_type=jnp.float32)
    return mixed + jnp.dot(left_high, right_high, preferred_element_type=jnp.float32)


def dot_full(left, right):
    return jnp.dot(left, right, precision=lax.Precision.HIGHEST, preferred_element_type=jnp.float32)


def shrink(error):
    return error * error / (2.0 - error * error)


def analyse_kernel(gram_ref, innov_ref, states_hbm, ids_hbm, out_ref, system_high, system_low, guess, answer,
                   states_ref, ids_ref, copy_sem):
    states_copy = pltpu.make_async_copy(states_hbm, states_ref, copy_sem.at[0])
    ids_copy = pltpu.make_async_copy(ids_hbm, ids_ref, copy_sem.at[1])
    states_copy.start()
    ids_copy.start()
    boxes, members, _ = gram_ref.shape
    fields, cells, _ = states_ref.shape
    rows = lax.broadcasted_iota(jnp.int32, (members, members), 0)
    columns = lax.broadcasted_iota(jnp.int32, (members, members), 1)
    identity = (rows == columns).astype(jnp.float32)
    ridge = members - 1.0

    worst = jnp.float32(0.0)
    errors = []
    for b in range(boxes):
        full = gram_ref[b] + ridge * identity
        top = jnp.maximum(jnp.max(jnp.sum(jnp.abs(full), axis=0, keepdims=True)), ridge)
        first = 2.0 / (top + ridge)
        error = (top - ridge) / (top + ridge)
        mu = 2.0 / (2.0 - error * error)
        high, low = split(full)
        system_high[b] = high
        system_low[b] = low
        start = (mu * first) * (2.0 * identity - first * full)
        guess[b] = start.astype(jnp.bfloat16)
        answer[b] = start
        errors.append(shrink(error))
        worst = jnp.maximum(worst, top / ridge)

    def coarse(carried):
        after = []
        for b in range(boxes):
            error = carried[b]
            mu = 2.0 / (2.0 - error * error)
            held = guess[b]
            left = identity - jnp.dot(system_high[b], held, preferred_element_type=jnp.float32)
            more = jnp.dot(held, left.astype(jnp.bfloat16), preferred_element_type=jnp.float32)
            guess[b] = (mu * (held.astype(jnp.float32) + more)).astype(jnp.bfloat16)
            after.append(shrink(error))
        return tuple(after)

    def refine(dot):
        def step(carried):
            after = []
            for b in range(boxes):
                error = carried[b]
                mu = 2.0 / (2.0 - error * error)
                full = gram_ref[b] + ridge * identity
                left = 2.0 * identity - dot(full, answer[b])
                answer[b] = mu * dot(answer[b], left)
                after.append(shrink(error))
            return tuple(after)
        return step

    def above(limit):
        def proceed(carried):
            top = carried[0]
            for error in carried[1:]:
                top = jnp.maximum(top, error)
            return top > limit
        return proceed

    easy = worst < 64.0
    hard = worst > 2048.0

    @pl.when(easy)
    def _():
        lax.while_loop(above(0.005), coarse, tuple(errors))
        for b in range(boxes):
            held = guess[b]
            left = identity - jnp.dot(system_high[b], held, preferred_element_type=jnp.float32)
            left = left - jnp.dot(system_low[b], held, preferred_element_type=jnp.float32)
            more = jnp.dot(held, left.astype(jnp.bfloat16), preferred_element_type=jnp.float32)
            answer[b] = held.astype(jnp.float32) + more

    @pl.when(jnp.logical_and(jnp.logical_not(easy), jnp.logical_not(hard)))
    def _():
        lax.while_loop(above(3e-4), refine(dot_thrice), tuple(errors))

    @pl.when(hard)
    def _():
        lax.while_loop(above(1e-6), refine(dot_full), tuple(errors))

    states_copy.wait()
    ids_copy.wait()
    wide = states_ref[...].astype(jnp.float32).reshape(fields * cells, members)
    smean = jnp.sum(wide, axis=1, keepdims=True) * (1.0 / members)
    anomaly = (wide - smean).astype(jnp.bfloat16)
    here = lax.broadcasted_iota(jnp.int32, (cells, cells), 0) == lax.broadcasted_iota(jnp.int32, (cells, cells), 1)
    spread = jnp.broadcast_to(ids_ref[...].astype(jnp.float32), (cells, cells))
    ids = jnp.sum(jnp.where(here, spread, 0.0), axis=1, keepdims=True)
    ids = jnp.concatenate([ids] * fields, axis=0)
    total = jnp.zeros((fields * cells, members), jnp.float32)
    for b in range(boxes):
        inverse = answer[b]
        wbar = jnp.sum(inverse * innov_ref[b:b + 1, :], axis=1, keepdims=True)
        transform = (0.5 * identity + (0.5 * ridge) * inverse + wbar).astype(jnp.bfloat16)
        update = jnp.dot(anomaly, transform, preferred_element_type=jnp.float32)
        total = jnp.where(ids == float(b), update, total)
    out_ref[...] = (smean + total).astype(jnp.bfloat16).reshape(fields, cells, members)


def analyse(gram, innov, states, box_ids):
    boxes, members, _ = gram.shape
    square = (boxes, members, members)
    return pl.pallas_call(
        analyse_kernel,
        out_shape=jax.ShapeDtypeStruct(states.shape, jnp.bfloat16),
        in_specs=[pl.BlockSpec(memory_space=pltpu.VMEM)] * 2 + [pl.BlockSpec(memory_space=pl.ANY)] * 2,
        out_specs=pl.BlockSpec(memory_space=pltpu.VMEM),
        scratch_shapes=[
            pltpu.VMEM(square, jnp.bfloat16),
            pltpu.VMEM(square, jnp.bfloat16),
            pltpu.VMEM(square, jnp.bfloat16),
            pltpu.VMEM(square, jnp.float32),
            pltpu.VMEM(states.shape, jnp.bfloat16),
            pltpu.VMEM((1, box_ids.shape[0]), jnp.int32),
            pltpu.SemaphoreType.DMA((2,)),
        ],
        compiler_params=pltpu.CompilerParams(vmem_limit_bytes=56 * 1024 * 1024),
        name="analyse",
    )(gram, innov, states, box_ids.reshape(1, -1))


def body(ens_obs, obs_values, obs_var, edge_up, edge_down, loc_local, loc_edge, states, box_ids):
    gram, innov = gathered_sums(ens_obs, obs_values, obs_var, edge_up, edge_down, loc_local, loc_edge)
    return analyse(gram, innov, states, box_ids)


def solution(mesh):
    return jax.shard_map(
        body,
        mesh=mesh,
        in_specs=(
            P(("region", "tile"), None),
            P(("region", "tile")),
            P(("region", "tile")),
            P(("region", "tile")),
            P(("region", "tile")),
            P(("region", "tile"), None),
            P(("region", "tile"), None),
            P(None, ("region", "tile"), None),
            P(("region", "tile")),
        ),
        out_specs=P(None, ("region", "tile"), None),
        check_vma=False,
    )
```

```python
import functools
import jax
import jax.numpy as jnp
from jax import lax
from jax.experimental import pallas as pl
from jax.experimental.pallas import tpu as pltpu
from jax.sharding import PartitionSpec as P


INFO_ROWS = 16
LANES = 128


def tile_sides(tiles):
    return 4, 2, tiles // 8


def gather_kernel(regions, tiles, ens_hbm, values_hbm, var_hbm, up_hbm, down_hbm, local_hbm, edge_hbm,
                  gram_ref, innov_ref, ens_ref, values_ref, var_ref, up_ref, down_ref, local_ref, edge_ref,
                  copy_sem, pool, near_weights, far_weights, leaving, arriving,
                  send_sem, recv_sem, edge_send_sem, edge_recv_sem):
    region = lax.axis_index("region")
    tile = lax.axis_index("tile")
    fetched = []
    for number, (far, near) in enumerate([
        (ens_hbm, ens_ref), (values_hbm, values_ref), (var_hbm, var_ref), (up_hbm, up_ref),
        (down_hbm, down_ref), (local_hbm, local_ref), (edge_hbm, edge_ref),
    ]):
        fetched.append(pltpu.make_async_copy(far, near, copy_sem.at[number]))
        fetched[-1].start()
    z_side, y_side, x_side = tile_sides(tiles)
    plane = y_side * x_side
    at_z, at_y, at_x = tile // plane, (tile // x_side) % y_side, tile % x_side
    at = tile % plane
    records, members = ens_ref.shape
    boxes = local_ref.shape[0]
    edges = up_ref.shape[1]
    sides = leaving.shape[0]
    block_rows = pool.shape[2]
    info_at = block_rows - INFO_ROWS
    parts = members // LANES
    cut = (block_rows // 2 + 15) // 16 * 16

    x_others = [at_y * x_side + (at_x + d) % x_side for d in range(1, x_side)]
    y_others = [(at_y + d) % y_side * x_side + at_x for d in range(1, y_side)]
    z_others = [(at_z + d) % z_side for d in range(1, z_side)]
    if sides == 1:
        partners = [1 - region]
    else:
        partners = [(region + 1) % regions, (region + regions - 1) % regions]

    barrier = pltpu.get_barrier_semaphore()
    greeted = [(region, z * plane + at) for z in z_others]
    greeted += [(region, at_z * plane + p) for p in x_others + y_others]
    greeted += [(partner, tile) for partner in partners]
    for device in greeted:
        pl.semaphore_signal(barrier, inc=1, device_id=device, device_id_type=pl.DeviceIdType.MESH)

    for copy in fetched[:5]:
        copy.wait()
    wide = ens_ref[...].astype(jnp.float32)
    ymean = jnp.sum(wide, axis=1, keepdims=True) * (1.0 / members)
    anomaly = (wide - ymean).astype(jnp.bfloat16)
    row_at = lax.broadcasted_iota(jnp.int32, (records, records), 0)
    column_at = lax.broadcasted_iota(jnp.int32, (records, records), 1)
    ymean_row = jnp.sum(jnp.where(row_at == column_at, ymean, 0.0), axis=0, keepdims=True)
    index_row = jnp.concatenate(
        [up_ref[...].astype(jnp.float32), down_ref[...].astype(jnp.float32),
         jnp.zeros((1, LANES - 2 * edges), jnp.float32)], axis=1)
    info = jnp.concatenate(
        [1.0 / var_ref[...], values_ref[...] - ymean_row, index_row,
         jnp.zeros((INFO_ROWS - 3, records), jnp.float32)], axis=0)
    for part in range(parts):
        pool[at, at_z, part * records:(part + 1) * records, :] = anomaly[:, part * LANES:(part + 1) * LANES]
    pool[at, at_z, info_at:, :] = info.astype(jnp.bfloat16)
    pl.semaphore_wait(barrier, len(greeted))
    started = []

    def piece(place, z, part):
        if part is None:
            return pool.at[place, z]
        if part == 0:
            return pool.at[place, z, pl.ds(0, cut)]
        return pool.at[place, z, pl.ds(cut, block_rows - cut)]

    def describe(place, z, part, device, number):
        return pltpu.make_async_remote_copy(
            src_ref=piece(place, z, part), dst_ref=piece(place, z, part),
            send_sem=send_sem.at[number], recv_sem=recv_sem.at[1 if part == 1 else 0, place, z],
            device_id=device, device_id_type=pl.DeviceIdType.MESH,
        )

    def send(place, z, part, device):
        copy = describe(place, z, part, device, len(started))
        copy.start()
        started.append(copy)

    def await_piece(place, z, part=None):
        describe(place, z, part, (region, tile), 0).wait_recv()

    def spread(z):
        for p in x_others + y_others:
            send(at, z, None, (region, at_z * plane + p))

    for z in z_others:
        send(at, at_z, None, (region, z * plane + at))
    spread(at_z)

    for copy in fetched[5:]:
        copy.wait()
    for t in range(tiles):
        near_weights[t] = local_ref[:, t * records:(t + 1) * records]
    for place in range(plane):
        columns = [(z * plane + place) * 2 * edges for z in range(z_side)]
        lower = jnp.concatenate([edge_ref[:, c:c + edges] for c in columns], axis=1)
        upper = jnp.concatenate([edge_ref[:, c + edges:c + 2 * edges] for c in columns], axis=1)
        if sides == 1:
            far_weights[0, place] = jnp.where(region == 0, upper, lower)
        else:
            far_weights[0, place] = lower
            far_weights[1, place] = upper

    def flat(block):
        return jnp.concatenate([block[part * records:(part + 1) * records] for part in range(parts)], axis=1)

    def add(data, inverse_var, innovation, loc, first=False):
        scale = loc * inverse_var
        weighted = (scale * innovation).astype(jnp.bfloat16)
        turned = data.astype(jnp.float32).T
        more = jnp.dot(weighted, data, preferred_element_type=jnp.float32)
        innov_ref[...] = more if first else innov_ref[...] + more
        for b in range(boxes):
            scaled = (turned * scale[b:b + 1]).astype(jnp.bfloat16)
            more = jnp.dot(scaled, data, preferred_element_type=jnp.float32)
            gram_ref[b] = more if first else gram_ref[b] + more

    def crossing(place, side):
        return pltpu.make_async_remote_copy(
            src_ref=leaving.at[side, place], dst_ref=arriving.at[side, place],
            send_sem=edge_send_sem.at[side, place], recv_sem=edge_recv_sem.at[side, place],
            device_id=(partners[side], tile), device_id_type=pl.DeviceIdType.MESH,
        )

    def near_group(place, first=False):
        data = jnp.concatenate([flat(pool[place, z]) for z in range(z_side)], axis=0)
        infos = [pool[place, z, info_at:, :] for z in range(z_side)]
        info = jnp.concatenate(infos, axis=1)
        wide_infos = [each.astype(jnp.float32) for each in infos]
        for side in range(sides):
            if sides == 1:
                index = [jnp.where(region == 0, each[2:3, :edges], each[2:3, edges:2 * edges]) for each in wide_infos]
                keep = 1.0
            else:
                index = [each[2:3, side * edges:(side + 1) * edges] for each in wide_infos]
                keep = jnp.where(region == (0 if side else regions - 1), 0.0, 1.0)
            index = jnp.concatenate([index[z] + float(z * records) for z in range(z_side)], axis=1)
            picked = z_side * edges
            row_of = lax.broadcasted_iota(jnp.int32, (z_side * records, picked), 0).astype(jnp.float32)
            chosen = jnp.where(row_of == index, keep, 0.0)
            far_info = jnp.dot(info, chosen.astype(jnp.bfloat16), preferred_element_type=jnp.float32)
            far = jnp.dot(chosen.T.astype(jnp.bfloat16), data, preferred_element_type=jnp.float32)
            far = far.astype(jnp.bfloat16)
            for part in range(parts):
                leaving[side, place, part * picked:(part + 1) * picked, :] = far[:, part * LANES:(part + 1) * LANES]
            leaving[side, place, parts * picked:, :] = far_info.astype(jnp.bfloat16)
            crossing(place, side).start()
        wide_info = info.astype(jnp.float32)
        loc = jnp.concatenate([near_weights[z * plane + place] for z in range(z_side)], axis=1)
        return lambda: add(data, wide_info[0:1], wide_info[1:2], loc, first)

    def far_groups(places):
        data, info, loc = [], [], []
        picked = z_side * edges
        for place in places:
            for side in range(sides):
                crossing(place, side).wait_recv()
                block = arriving[side, place]
                data.append(jnp.concatenate(
                    [block[part * picked:(part + 1) * picked] for part in range(parts)], axis=1))
                info.append(block[parts * picked:].astype(jnp.float32))
                loc.append(far_weights[side, place])
        data = jnp.concatenate(data, axis=0)
        info = jnp.concatenate(info, axis=1)
        add(data, info[0:1], info[1:2], jnp.concatenate(loc, axis=1))

    order = [(at_z + z_side - d) % z_side for d in range(1, z_side)]
    for z in order:
        await_piece(at, z)
        spread(z)
    near_group(at, first=True)()
    for z in [at_z] + order:
        for p in x_others:
            await_piece(p, z)
            for d in range(1, y_side):
                far = (at_y + d) % y_side * x_side + at_x
                send(p, z, 0, (region, at_z * plane + far))
        for p in y_others:
            await_piece(p, z)
            for d in range(1, x_side):
                far = at_y * x_side + (at_x + d) % x_side
                send(p, z, 1, (region, at_z * plane + far))
    for p in x_others + y_others:
        near_group(p)()
    far_groups([at] + x_others + y_others)
    diagonal = [
        (at_y + dy) % y_side * x_side + (at_x + dx) % x_side
        for dy in range(1, y_side) for dx in range(1, x_side)
    ]
    for far in diagonal:
        for z in [at_z] + order:
            await_piece(far, z, 0)
            await_piece(far, z, 1)
        near_group(far)()
    far_groups(diagonal)
    for place in [at] + x_others + y_others + diagonal:
        for side in range(sides):
            crossing(place, side).wait_send()
    for copy in started:
        copy.wait_send()


def gathered_sums(ens_obs, obs_values, obs_var, edge_up, edge_down, loc_local, loc_edge):
    regions, tiles = lax.axis_size("region"), lax.axis_size("tile")
    records, members = ens_obs.shape
    boxes, edges = loc_local.shape[0], edge_up.shape[0]
    sides = 1 if regions == 2 else 2
    z_side, y_side, x_side = tile_sides(tiles)
    plane = y_side * x_side
    block_rows = members // LANES * records + INFO_ROWS
    edge_rows = members // LANES * z_side * edges + INFO_ROWS
    sends = z_side - 1 + z_side * (x_side + y_side - 2) + 2 * z_side * (x_side - 1) * (y_side - 1)
    arrays = (ens_obs, obs_values.reshape(1, -1), obs_var.reshape(1, -1), edge_up.reshape(1, -1),
              edge_down.reshape(1, -1), loc_local, loc_edge)
    return pl.pallas_call(
        functools.partial(gather_kernel, regions, tiles),
        out_shape=(
            jax.ShapeDtypeStruct((boxes, members, members), jnp.float32),
            jax.ShapeDtypeStruct((boxes, members), jnp.float32),
        ),
        in_specs=[pl.BlockSpec(memory_space=pl.ANY)] * 7,
        out_specs=[pl.BlockSpec(memory_space=pltpu.VMEM)] * 2,
        scratch_shapes=[pltpu.VMEM(array.shape, array.dtype) for array in arrays] + [
            pltpu.SemaphoreType.DMA((len(arrays),)),
            pltpu.VMEM((plane, z_side, block_rows, LANES), jnp.bfloat16),
            pltpu.VMEM((tiles, boxes, records), jnp.float32),
            pltpu.VMEM((sides, plane, boxes, z_side * edges), jnp.float32),
            pltpu.VMEM((sides, plane, edge_rows, LANES), jnp.bfloat16),
            pltpu.VMEM((sides, plane, edge_rows, LANES), jnp.bfloat16),
            pltpu.SemaphoreType.DMA((sends,)),
            pltpu.SemaphoreType.DMA((2, plane, z_side)),
            pltpu.SemaphoreType.DMA((sides, plane)),
            pltpu.SemaphoreType.DMA((sides, plane)),
        ],
        compiler_params=pltpu.CompilerParams(
            collective_id=0, has_side_effects=True, vmem_limit_bytes=56 * 1024 * 1024
        ),
        name="gather_gram",
    )(*arrays)


def split(x):
    high = x.astype(jnp.bfloat16)
    return high, (x - high.astype(jnp.float32)).astype(jnp.bfloat16)


def dot_thrice(left, right):
    left_high, left_low = split(left)
    right_high, right_low = split(right)
    mixed = jnp.dot(left_low, right_high, preferred_element_type=jnp.float32)
    mixed += jnp.dot(left_high, right_low, preferred_element_type=jnp.float32)
    return mixed + jnp.dot(left_high, right_high, preferred_element_type=jnp.float32)


def dot_full(left, right):
    return jnp.dot(left, right, precision=lax.Precision.HIGHEST, preferred_element_type=jnp.float32)


def shrink(error):
    return error * error / (2.0 - error * error)


def analyse_kernel(gram_ref, innov_ref, states_hbm, ids_hbm, out_ref, system_high, system_low, guess, answer,
                   states_ref, ids_ref, copy_sem):
    states_copy = pltpu.make_async_copy(states_hbm, states_ref, copy_sem.at[0])
    ids_copy = pltpu.make_async_copy(ids_hbm, ids_ref, copy_sem.at[1])
    states_copy.start()
    ids_copy.start()
    boxes, members, _ = gram_ref.shape
    fields, cells, _ = states_ref.shape
    rows = lax.broadcasted_iota(jnp.int32, (members, members), 0)
    columns = lax.broadcasted_iota(jnp.int32, (members, members), 1)
    identity = (rows == columns).astype(jnp.float32)
    ridge = members - 1.0

    worst = jnp.float32(0.0)
    errors = []
    for b in range(boxes):
        full = gram_ref[b] + ridge * identity
        top = jnp.maximum(jnp.max(jnp.sum(jnp.abs(full), axis=0, keepdims=True)), ridge)
        first = 2.0 / (top + ridge)
        error = (top - ridge) / (top + ridge)
        mu = 2.0 / (2.0 - error * error)
        high, low = split(full)
        system_high[b] = high
        system_low[b] = low
        start = (mu * first) * (2.0 * identity - first * full)
        guess[b] = start.astype(jnp.bfloat16)
        answer[b] = start
        errors.append(shrink(error))
        worst = jnp.maximum(worst, top / ridge)

    def coarse(carried):
        after = []
        for b in range(boxes):
            error = carried[b]
            mu = 2.0 / (2.0 - error * error)
            held = guess[b]
            left = identity - jnp.dot(system_high[b], held, preferred_element_type=jnp.float32)
            more = jnp.dot(held, left.astype(jnp.bfloat16), preferred_element_type=jnp.float32)
            guess[b] = (mu * (held.astype(jnp.float32) + more)).astype(jnp.bfloat16)
            after.append(shrink(error))
        return tuple(after)

    def refine(dot):
        def step(carried):
            after = []
            for b in range(boxes):
                error = carried[b]
                mu = 2.0 / (2.0 - error * error)
                full = gram_ref[b] + ridge * identity
                left = 2.0 * identity - dot(full, answer[b])
                answer[b] = mu * dot(answer[b], left)
                after.append(shrink(error))
            return tuple(after)
        return step

    def above(limit):
        def proceed(carried):
            top = carried[0]
            for error in carried[1:]:
                top = jnp.maximum(top, error)
            return top > limit
        return proceed

    easy = worst < 64.0
    hard = worst > 2048.0

    @pl.when(easy)
    def _():
        lax.while_loop(above(0.02), coarse, tuple(errors))
        for b in range(boxes):
            held = guess[b]
            left = identity - jnp.dot(system_high[b], held, preferred_element_type=jnp.float32)
            left = left - jnp.dot(system_low[b], held, preferred_element_type=jnp.float32)
            more = jnp.dot(held, left.astype(jnp.bfloat16), preferred_element_type=jnp.float32)
            answer[b] = held.astype(jnp.float32) + more

    @pl.when(jnp.logical_and(jnp.logical_not(easy), jnp.logical_not(hard)))
    def _():
        lax.while_loop(above(3e-4), refine(dot_thrice), tuple(errors))

    @pl.when(hard)
    def _():
        lax.while_loop(above(1e-6), refine(dot_full), tuple(errors))

    states_copy.wait()
    ids_copy.wait()
    wide = states_ref[...].astype(jnp.float32).reshape(fields * cells, members)
    smean = jnp.sum(wide, axis=1, keepdims=True) * (1.0 / members)
    anomaly = (wide - smean).astype(jnp.bfloat16)
    here = lax.broadcasted_iota(jnp.int32, (cells, cells), 0) == lax.broadcasted_iota(jnp.int32, (cells, cells), 1)
    spread = jnp.broadcast_to(ids_ref[...].astype(jnp.float32), (cells, cells))
    ids = jnp.sum(jnp.where(here, spread, 0.0), axis=1, keepdims=True)
    ids = jnp.concatenate([ids] * fields, axis=0)
    total = jnp.zeros((fields * cells, members), jnp.float32)
    for b in range(boxes):
        inverse = answer[b]
        wbar = jnp.sum(inverse * innov_ref[b:b + 1, :], axis=1, keepdims=True)
        transform = (0.5 * identity + (0.5 * ridge) * inverse + wbar).astype(jnp.bfloat16)
        update = jnp.dot(anomaly, transform, preferred_element_type=jnp.float32)
        total = jnp.where(ids == float(b), update, total)
    out_ref[...] = (smean + total).astype(jnp.bfloat16).reshape(fields, cells, members)


def analyse(gram, innov, states, box_ids):
    boxes, members, _ = gram.shape
    square = (boxes, members, members)
    return pl.pallas_call(
        analyse_kernel,
        out_shape=jax.ShapeDtypeStruct(states.shape, jnp.bfloat16),
        in_specs=[pl.BlockSpec(memory_space=pltpu.VMEM)] * 2 + [pl.BlockSpec(memory_space=pl.ANY)] * 2,
        out_specs=pl.BlockSpec(memory_space=pltpu.VMEM),
        scratch_shapes=[
            pltpu.VMEM(square, jnp.bfloat16),
            pltpu.VMEM(square, jnp.bfloat16),
            pltpu.VMEM(square, jnp.bfloat16),
            pltpu.VMEM(square, jnp.float32),
            pltpu.VMEM(states.shape, jnp.bfloat16),
            pltpu.VMEM((1, box_ids.shape[0]), jnp.int32),
            pltpu.SemaphoreType.DMA((2,)),
        ],
        compiler_params=pltpu.CompilerParams(vmem_limit_bytes=56 * 1024 * 1024),
        name="analyse",
    )(gram, innov, states, box_ids.reshape(1, -1))


def body(ens_obs, obs_values, obs_var, edge_up, edge_down, loc_local, loc_edge, states, box_ids):
    gram, innov = gathered_sums(ens_obs, obs_values, obs_var, edge_up, edge_down, loc_local, loc_edge)
    return analyse(gram, innov, states, box_ids)


def solution(mesh):
    return jax.shard_map(
        body,
        mesh=mesh,
        in_specs=(
            P(("region", "tile"), None),
            P(("region", "tile")),
            P(("region", "tile")),
            P(("region", "tile")),
            P(("region", "tile")),
            P(("region", "tile"), None),
            P(("region", "tile"), None),
            P(None, ("region", "tile"), None),
            P(("region", "tile")),
        ),
        out_specs=P(None, ("region", "tile"), None),
        check_vma=False,
    )
```

```python
import functools
import jax
import jax.numpy as jnp
from jax import lax
from jax.experimental import pallas as pl
from jax.experimental.pallas import tpu as pltpu
from jax.sharding import PartitionSpec as P


INFO_ROWS = 16
LANES = 128
UNIT = 4


def tile_sides(tiles):
    return 4, 2, tiles // 8


def gather_kernel(regions, tiles, ens_hbm, values_hbm, var_hbm, up_hbm, down_hbm, local_hbm, edge_hbm,
                  gram_ref, innov_ref, ens_ref, values_ref, var_ref, up_ref, down_ref, local_ref, edge_ref,
                  copy_sem, pool, near_weights, far_weights, leaving, arriving,
                  send_sem, recv_sem, edge_send_sem, edge_recv_sem):
    region = lax.axis_index("region")
    tile = lax.axis_index("tile")
    fetched = []
    for number, (far, near) in enumerate([
        (ens_hbm, ens_ref), (values_hbm, values_ref), (var_hbm, var_ref), (up_hbm, up_ref),
        (down_hbm, down_ref), (local_hbm, local_ref), (edge_hbm, edge_ref),
    ]):
        fetched.append(pltpu.make_async_copy(far, near, copy_sem.at[number]))
        fetched[-1].start()
    z_side, y_side, x_side = tile_sides(tiles)
    plane = y_side * x_side
    at_z, at_y, at_x = tile // plane, (tile // x_side) % y_side, tile % x_side
    at = tile % plane
    records, members = ens_ref.shape
    boxes = local_ref.shape[0]
    edges = up_ref.shape[1]
    sides = leaving.shape[0]
    block_rows = pool.shape[2]
    info_at = block_rows - INFO_ROWS
    parts = members // LANES
    cut = (block_rows // 2 + 15) // 16 * 16

    x_others = [at_y * x_side + (at_x + d) % x_side for d in range(1, x_side)]
    y_others = [(at_y + d) % y_side * x_side + at_x for d in range(1, y_side)]
    z_others = [(at_z + d) % z_side for d in range(1, z_side)]
    if sides == 1:
        partners = [1 - region]
    else:
        partners = [(region + 1) % regions, (region + regions - 1) % regions]

    barrier = pltpu.get_barrier_semaphore()
    greeted = [(region, z * plane + at) for z in z_others]
    greeted += [(region, at_z * plane + p) for p in x_others + y_others]
    greeted += [(partner, tile) for partner in partners]
    for device in greeted:
        pl.semaphore_signal(barrier, inc=1, device_id=device, device_id_type=pl.DeviceIdType.MESH)

    for copy in fetched[:5]:
        copy.wait()
    wide = ens_ref[...].astype(jnp.float32)
    ymean = jnp.sum(wide, axis=1, keepdims=True) * (1.0 / members)
    anomaly = (wide - ymean).astype(jnp.bfloat16)
    row_at = lax.broadcasted_iota(jnp.int32, (records, records), 0)
    column_at = lax.broadcasted_iota(jnp.int32, (records, records), 1)
    ymean_row = jnp.sum(jnp.where(row_at == column_at, ymean, 0.0), axis=0, keepdims=True)
    index_row = jnp.concatenate(
        [up_ref[...].astype(jnp.float32), down_ref[...].astype(jnp.float32),
         jnp.zeros((1, LANES - 2 * edges), jnp.float32)], axis=1)
    info = jnp.concatenate(
        [1.0 / var_ref[...], values_ref[...] - ymean_row, index_row,
         jnp.zeros((INFO_ROWS - 3, records), jnp.float32)], axis=0)
    for part in range(parts):
        pool[at, at_z, part * records:(part + 1) * records, :] = anomaly[:, part * LANES:(part + 1) * LANES]
    pool[at, at_z, info_at:, :] = info.astype(jnp.bfloat16)
    pl.semaphore_wait(barrier, len(greeted))
    started = []

    def piece(place, z, part):
        if part is None:
            return pool.at[place, z]
        if part == 0:
            return pool.at[place, z, pl.ds(0, cut)]
        return pool.at[place, z, pl.ds(cut, block_rows - cut)]

    def describe(place, z, part, device, number):
        return pltpu.make_async_remote_copy(
            src_ref=piece(place, z, part), dst_ref=piece(place, z, part),
            send_sem=send_sem.at[number], recv_sem=recv_sem.at[1 if part == 1 else 0, place, z],
            device_id=device, device_id_type=pl.DeviceIdType.MESH,
        )

    def send(place, z, part, device):
        copy = describe(place, z, part, device, len(started))
        copy.start()
        started.append(copy)

    def await_piece(place, z, part=None):
        describe(place, z, part, (region, tile), 0).wait_recv()

    def spread(z):
        for p in x_others + y_others:
            send(at, z, None, (region, at_z * plane + p))

    for z in z_others:
        send(at, at_z, None, (region, z * plane + at))
    spread(at_z)

    for copy in fetched[5:]:
        copy.wait()
    for t in range(tiles):
        near_weights[t] = local_ref[:, t * records:(t + 1) * records]
        lower = edge_ref[:, 2 * t * edges:(2 * t + 1) * edges]
        upper = edge_ref[:, (2 * t + 1) * edges:(2 * t + 2) * edges]
        if sides == 1:
            far_weights[0, t] = jnp.where(region == 0, upper, lower)
        else:
            far_weights[0, t] = lower
            far_weights[1, t] = upper

    def flat(block, count):
        return jnp.concatenate([block[part * count:(part + 1) * count] for part in range(parts)], axis=1)

    def add(data, inverse_var, innovation, loc, first=False):
        scale = loc * inverse_var
        weighted = (scale * innovation).astype(jnp.bfloat16)
        turned = data.astype(jnp.float32).T
        more = jnp.dot(weighted, data, preferred_element_type=jnp.float32)
        innov_ref[...] = more if first else innov_ref[...] + more
        for b in range(boxes):
            scaled = (turned * scale[b:b + 1]).astype(jnp.bfloat16)
            more = jnp.dot(scaled, data, preferred_element_type=jnp.float32)
            gram_ref[b] = more if first else gram_ref[b] + more

    units = []

    def crossing(unit, side):
        extent = pl.ds(0, parts * len(units[unit]) * edges + INFO_ROWS)
        return pltpu.make_async_remote_copy(
            src_ref=leaving.at[side, unit, extent], dst_ref=arriving.at[side, unit, extent],
            send_sem=edge_send_sem.at[side, unit], recv_sem=edge_recv_sem.at[side, unit],
            device_id=(partners[side], tile), device_id_type=pl.DeviceIdType.MESH,
        )

    def near_unit(blocks):
        unit = len(units)
        units.append(blocks)
        data = jnp.concatenate([flat(pool[place, z], records) for place, z in blocks], axis=0)
        infos = [pool[place, z, info_at:, :] for place, z in blocks]
        info = jnp.concatenate(infos, axis=1)
        index_rows = [each.astype(jnp.float32)[2:3] for each in infos]
        picked = len(blocks) * edges
        for side in range(sides):
            if sides == 1:
                index = [jnp.where(region == 0, each[:, :edges], each[:, edges:2 * edges]) for each in index_rows]
                keep = 1.0
            else:
                index = [each[:, side * edges:(side + 1) * edges] for each in index_rows]
                keep = jnp.where(region == (0 if side else regions - 1), 0.0, 1.0)
            index = jnp.concatenate([each + float(n * records) for n, each in enumerate(index)], axis=1)
            index = jnp.concatenate([index, jnp.full((1, LANES - picked), -1.0, jnp.float32)], axis=1) if picked < LANES else index
            row_of = lax.broadcasted_iota(jnp.int32, (len(blocks) * records, LANES), 0).astype(jnp.float32)
            chosen = jnp.where(row_of == index, keep, 0.0)
            far_info = jnp.dot(info, chosen.astype(jnp.bfloat16), preferred_element_type=jnp.float32)
            far = jnp.dot(chosen.T[:picked].astype(jnp.bfloat16), data, preferred_element_type=jnp.float32)
            far = far.astype(jnp.bfloat16)
            for part in range(parts):
                leaving[side, unit, part * picked:(part + 1) * picked, :] = far[:, part * LANES:(part + 1) * LANES]
            leaving[side, unit, parts * picked:parts * picked + INFO_ROWS, :] = far_info.astype(jnp.bfloat16)
            crossing(unit, side).start()
        wide_info = info.astype(jnp.float32)
        loc = jnp.concatenate([near_weights[z * plane + place] for place, z in blocks], axis=1)
        add(data, wide_info[0:1], wide_info[1:2], loc, unit == 0)

    def near_units(blocks):
        for start in range(0, len(blocks), UNIT):
            near_unit(blocks[start:start + UNIT])

    def far_units(first, last):
        data, info, loc = [], [], []
        for unit in range(first, last):
            picked = len(units[unit]) * edges
            for side in range(sides):
                crossing(unit, side).wait_recv()
                data.append(flat(arriving[side, unit, :parts * picked, :], picked))
                info.append(arriving[side, unit, parts * picked:parts * picked + INFO_ROWS, :].astype(jnp.float32)[:, :picked])
                loc += [far_weights[side, z * plane + place] for place, z in units[unit]]
        data = jnp.concatenate(data, axis=0)
        info = jnp.concatenate(info, axis=1)
        add(data, info[0:1], info[1:2], jnp.concatenate(loc, axis=1))

    order = [(at_z + z_side - d) % z_side for d in range(1, z_side)]
    for z in order:
        await_piece(at, z)
        spread(z)
    order = [at_z] + order
    near_units([(at, z) for z in order])
    for z in order:
        for p in x_others:
            await_piece(p, z)
            for d in range(1, y_side):
                far = (at_y + d) % y_side * x_side + at_x
                send(p, z, 0, (region, at_z * plane + far))
        for p in y_others:
            await_piece(p, z)
            for d in range(1, x_side):
                far = at_y * x_side + (at_x + d) % x_side
                send(p, z, 1, (region, at_z * plane + far))
        near_units([(p, z) for p in x_others + y_others])
    early = len(units)
    far_units(0, early)
    diagonal = [
        (at_y + dy) % y_side * x_side + (at_x + dx) % x_side
        for dy in range(1, y_side) for dx in range(1, x_side)
    ]
    for start in range(0, z_side, 2):
        blocks = [(far, z) for far in diagonal for z in order[start:start + 2]]
        for far, z in blocks:
            await_piece(far, z, 0)
            await_piece(far, z, 1)
        near_units(blocks)
    far_units(early, len(units))
    for unit in range(len(units)):
        for side in range(sides):
            crossing(unit, side).wait_send()
    for copy in started:
        copy.wait_send()


def gathered_sums(ens_obs, obs_values, obs_var, edge_up, edge_down, loc_local, loc_edge):
    regions, tiles = lax.axis_size("region"), lax.axis_size("tile")
    records, members = ens_obs.shape
    boxes, edges = loc_local.shape[0], edge_up.shape[0]
    sides = 1 if regions == 2 else 2
    z_side, y_side, x_side = tile_sides(tiles)
    plane = y_side * x_side
    block_rows = members // LANES * records + INFO_ROWS
    edge_rows = members // LANES * UNIT * edges + INFO_ROWS
    sideways = x_side + y_side - 2
    corners = (x_side - 1) * (y_side - 1)
    units = 1 + z_side * (-(-sideways // UNIT)) + z_side // 2 * (-(-2 * corners // UNIT))
    sends = z_side - 1 + z_side * (x_side + y_side - 2) + 2 * z_side * (x_side - 1) * (y_side - 1)
    arrays = (ens_obs, obs_values.reshape(1, -1), obs_var.reshape(1, -1), edge_up.reshape(1, -1),
              edge_down.reshape(1, -1), loc_local, loc_edge)
    return pl.pallas_call(
        functools.partial(gather_kernel, regions, tiles),
        out_shape=(
            jax.ShapeDtypeStruct((boxes, members, members), jnp.float32),
            jax.ShapeDtypeStruct((boxes, members), jnp.float32),
        ),
        in_specs=[pl.BlockSpec(memory_space=pl.ANY)] * 7,
        out_specs=[pl.BlockSpec(memory_space=pltpu.VMEM)] * 2,
        scratch_shapes=[pltpu.VMEM(array.shape, array.dtype) for array in arrays] + [
            pltpu.SemaphoreType.DMA((len(arrays),)),
            pltpu.VMEM((plane, z_side, block_rows, LANES), jnp.bfloat16),
            pltpu.VMEM((tiles, boxes, records), jnp.float32),
            pltpu.VMEM((sides, tiles, boxes, edges), jnp.float32),
            pltpu.VMEM((sides, units, edge_rows, LANES), jnp.bfloat16),
            pltpu.VMEM((sides, units, edge_rows, LANES), jnp.bfloat16),
            pltpu.SemaphoreType.DMA((sends,)),
            pltpu.SemaphoreType.DMA((2, plane, z_side)),
            pltpu.SemaphoreType.DMA((sides, units)),
            pltpu.SemaphoreType.DMA((sides, units)),
        ],
        compiler_params=pltpu.CompilerParams(
            collective_id=0, has_side_effects=True, vmem_limit_bytes=56 * 1024 * 1024
        ),
        name="gather_gram",
    )(*arrays)


def split(x):
    high = x.astype(jnp.bfloat16)
    return high, (x - high.astype(jnp.float32)).astype(jnp.bfloat16)


def dot_thrice(left, right):
    left_high, left_low = split(left)
    right_high, right_low = split(right)
    mixed = jnp.dot(left_low, right_high, preferred_element_type=jnp.float32)
    mixed += jnp.dot(left_high, right_low, preferred_element_type=jnp.float32)
    return mixed + jnp.dot(left_high, right_high, preferred_element_type=jnp.float32)


def dot_full(left, right):
    return jnp.dot(left, right, precision=lax.Precision.HIGHEST, preferred_element_type=jnp.float32)


def shrink(error):
    return error * error / (2.0 - error * error)


def analyse_kernel(gram_hbm, innov_ref, states_hbm, ids_hbm, out_ref, system_high, system_low, guess, answer,
                   gram_ref, states_ref, ids_ref, copy_sem):
    states_copy = pltpu.make_async_copy(states_hbm, states_ref, copy_sem.at[0])
    ids_copy = pltpu.make_async_copy(ids_hbm, ids_ref, copy_sem.at[1])
    states_copy.start()
    ids_copy.start()
    gram_copies = [
        pltpu.make_async_copy(gram_hbm.at[b], gram_ref.at[b], copy_sem.at[2 + b]) for b in range(gram_ref.shape[0])
    ]
    for copy in gram_copies:
        copy.start()
    boxes, members, _ = gram_ref.shape
    fields, cells, _ = states_ref.shape
    rows = lax.broadcasted_iota(jnp.int32, (members, members), 0)
    columns = lax.broadcasted_iota(jnp.int32, (members, members), 1)
    identity = (rows == columns).astype(jnp.float32)
    ridge = members - 1.0

    states_copy.wait()
    ids_copy.wait()
    wide = states_ref[...].astype(jnp.float32).reshape(fields * cells, members)
    smean = jnp.sum(wide, axis=1, keepdims=True) * (1.0 / members)
    anomaly = (wide - smean).astype(jnp.bfloat16)
    here = lax.broadcasted_iota(jnp.int32, (cells, cells), 0) == lax.broadcasted_iota(jnp.int32, (cells, cells), 1)
    spread = jnp.broadcast_to(ids_ref[...].astype(jnp.float32), (cells, cells))
    ids = jnp.sum(jnp.where(here, spread, 0.0), axis=1, keepdims=True)
    ids = jnp.concatenate([ids] * fields, axis=0)

    worst = jnp.float32(0.0)
    errors = []
    for b in range(boxes):
        gram_copies[b].wait()
        full = gram_ref[b] + ridge * identity
        top = jnp.maximum(jnp.max(jnp.sum(jnp.abs(full), axis=0, keepdims=True)), ridge)
        first = 2.0 / (top + ridge)
        error = (top - ridge) / (top + ridge)
        mu = 2.0 / (2.0 - error * error)
        high, low = split(full)
        system_high[b] = high
        system_low[b] = low
        start = (mu * first) * (2.0 * identity - first * full)
        guess[b] = start.astype(jnp.bfloat16)
        answer[b] = start
        errors.append(shrink(error))
        worst = jnp.maximum(worst, top / ridge)

    def coarse(carried):
        after = []
        for b in range(boxes):
            error = carried[b]
            mu = 2.0 / (2.0 - error * error)
            held = guess[b]
            left = identity - jnp.dot(system_high[b], held, preferred_element_type=jnp.float32)
            more = jnp.dot(held, left.astype(jnp.bfloat16), preferred_element_type=jnp.float32)
            guess[b] = (mu * (held.astype(jnp.float32) + more)).astype(jnp.bfloat16)
            after.append(shrink(error))
        return tuple(after)

    def refine(dot):
        def step(carried):
            after = []
            for b in range(boxes):
                error = carried[b]
                mu = 2.0 / (2.0 - error * error)
                full = gram_ref[b] + ridge * identity
                left = 2.0 * identity - dot(full, answer[b])
                answer[b] = mu * dot(answer[b], left)
                after.append(shrink(error))
            return tuple(after)
        return step

    def above(limit):
        def proceed(carried):
            top = carried[0]
            for error in carried[1:]:
                top = jnp.maximum(top, error)
            return top > limit
        return proceed

    easy = worst < 64.0
    hard = worst > 2048.0

    @pl.when(easy)
    def _():
        lax.while_loop(above(0.02), coarse, tuple(errors))
        for b in range(boxes):
            held = guess[b]
            left = identity - jnp.dot(system_high[b], held, preferred_element_type=jnp.float32)
            left = left - jnp.dot(system_low[b], held, preferred_element_type=jnp.float32)
            more = jnp.dot(held, left.astype(jnp.bfloat16), preferred_element_type=jnp.float32)
            answer[b] = held.astype(jnp.float32) + more

    @pl.when(jnp.logical_and(jnp.logical_not(easy), jnp.logical_not(hard)))
    def _():
        lax.while_loop(above(3e-4), refine(dot_thrice), tuple(errors))

    @pl.when(hard)
    def _():
        lax.while_loop(above(1e-6), refine(dot_full), tuple(errors))

    total = jnp.zeros((fields * cells, members), jnp.float32)
    for b in range(boxes):
        inverse = answer[b]
        wbar = jnp.sum(inverse * innov_ref[b:b + 1, :], axis=1, keepdims=True)
        transform = (0.5 * identity + (0.5 * ridge) * inverse + wbar).astype(jnp.bfloat16)
        update = jnp.dot(anomaly, transform, preferred_element_type=jnp.float32)
        total = jnp.where(ids == float(b), update, total)
    out_ref[...] = (smean + total).astype(jnp.bfloat16).reshape(fields, cells, members)


def analyse(gram, innov, states, box_ids):
    boxes, members, _ = gram.shape
    square = (boxes, members, members)
    return pl.pallas_call(
        analyse_kernel,
        out_shape=jax.ShapeDtypeStruct(states.shape, jnp.bfloat16),
        in_specs=[
            pl.BlockSpec(memory_space=pl.ANY), pl.BlockSpec(memory_space=pltpu.VMEM),
            pl.BlockSpec(memory_space=pl.ANY), pl.BlockSpec(memory_space=pl.ANY),
        ],
        out_specs=pl.BlockSpec(memory_space=pltpu.VMEM),
        scratch_shapes=[
            pltpu.VMEM(square, jnp.bfloat16),
            pltpu.VMEM(square, jnp.bfloat16),
            pltpu.VMEM(square, jnp.bfloat16),
            pltpu.VMEM(square, jnp.float32),
            pltpu.VMEM(square, jnp.float32),
            pltpu.VMEM(states.shape, jnp.bfloat16),
            pltpu.VMEM((1, box_ids.shape[0]), jnp.int32),
            pltpu.SemaphoreType.DMA((2 + boxes,)),
        ],
        compiler_params=pltpu.CompilerParams(vmem_limit_bytes=56 * 1024 * 1024),
        name="analyse",
    )(gram, innov, states, box_ids.reshape(1, -1))


def body(ens_obs, obs_values, obs_var, edge_up, edge_down, loc_local, loc_edge, states, box_ids):
    gram, innov = gathered_sums(ens_obs, obs_values, obs_var, edge_up, edge_down, loc_local, loc_edge)
    return analyse(gram, innov, states, box_ids)


def solution(mesh):
    return jax.shard_map(
        body,
        mesh=mesh,
        in_specs=(
            P(("region", "tile"), None),
            P(("region", "tile")),
            P(("region", "tile")),
            P(("region", "tile")),
            P(("region", "tile")),
            P(("region", "tile"), None),
            P(("region", "tile"), None),
            P(None, ("region", "tile"), None),
            P(("region", "tile")),
        ),
        out_specs=P(None, ("region", "tile"), None),
        check_vma=False,
    )
```

```python
import functools
import jax
import jax.numpy as jnp
from jax import lax
from jax.experimental import pallas as pl
from jax.experimental.pallas import tpu as pltpu
from jax.sharding import PartitionSpec as P


INFO_ROWS = 16
LANES = 128
UNIT = 4


def tile_sides(tiles):
    return 4, 2, tiles // 8


def gather_kernel(regions, tiles, ens_hbm, values_hbm, var_hbm, up_hbm, down_hbm, local_hbm, edge_hbm,
                  gram_ref, innov_ref, ens_ref, values_ref, var_ref, up_ref, down_ref, local_ref, edge_ref,
                  copy_sem, pool, near_weights, far_weights, leaving, arriving,
                  send_sem, recv_sem, edge_send_sem, edge_recv_sem):
    region = lax.axis_index("region")
    tile = lax.axis_index("tile")
    fetched = []
    for number, (far, near) in enumerate([
        (ens_hbm, ens_ref), (values_hbm, values_ref), (var_hbm, var_ref), (up_hbm, up_ref),
        (down_hbm, down_ref), (local_hbm, local_ref), (edge_hbm, edge_ref),
    ]):
        fetched.append(pltpu.make_async_copy(far, near, copy_sem.at[number]))
        fetched[-1].start()
    z_side, y_side, x_side = tile_sides(tiles)
    plane = y_side * x_side
    at_z, at_y, at_x = tile // plane, (tile // x_side) % y_side, tile % x_side
    at = tile % plane
    records, members = ens_ref.shape
    boxes = local_ref.shape[0]
    edges = up_ref.shape[1]
    sides = leaving.shape[0]
    block_rows = pool.shape[2]
    info_at = block_rows - INFO_ROWS
    parts = members // LANES
    cut = (block_rows // 2 + 15) // 16 * 16

    x_others = [at_y * x_side + (at_x + d) % x_side for d in range(1, x_side)]
    y_others = [(at_y + d) % y_side * x_side + at_x for d in range(1, y_side)]
    z_others = [at_z + 1 - 2 * (at_z % 2), (at_z + 2) % z_side, z_side - 1 - at_z]
    if sides == 1:
        partners = [1 - region]
    else:
        partners = [(region + 1) % regions, (region + regions - 1) % regions]

    barrier = pltpu.get_barrier_semaphore()
    greeted = [(region, z * plane + at) for z in z_others]
    greeted += [(region, at_z * plane + p) for p in x_others + y_others]
    greeted += [(partner, tile) for partner in partners]
    for device in greeted:
        pl.semaphore_signal(barrier, inc=1, device_id=device, device_id_type=pl.DeviceIdType.MESH)

    for copy in fetched[:5]:
        copy.wait()
    wide = ens_ref[...].astype(jnp.float32)
    ymean = jnp.sum(wide, axis=1, keepdims=True) * (1.0 / members)
    anomaly = (wide - ymean).astype(jnp.bfloat16)
    row_at = lax.broadcasted_iota(jnp.int32, (records, records), 0)
    column_at = lax.broadcasted_iota(jnp.int32, (records, records), 1)
    ymean_row = jnp.sum(jnp.where(row_at == column_at, ymean, 0.0), axis=0, keepdims=True)
    index_row = jnp.concatenate(
        [up_ref[...].astype(jnp.float32), down_ref[...].astype(jnp.float32),
         jnp.zeros((1, LANES - 2 * edges), jnp.float32)], axis=1)
    info = jnp.concatenate(
        [1.0 / var_ref[...], values_ref[...] - ymean_row, index_row,
         jnp.zeros((INFO_ROWS - 3, records), jnp.float32)], axis=0)
    for part in range(parts):
        pool[at, at_z, part * records:(part + 1) * records, :] = anomaly[:, part * LANES:(part + 1) * LANES]
    pool[at, at_z, info_at:, :] = info.astype(jnp.bfloat16)
    pl.semaphore_wait(barrier, len(greeted))
    started = []

    def piece(place, z, part):
        if part is None:
            return pool.at[place, z]
        if part == 0:
            return pool.at[place, z, pl.ds(0, cut)]
        return pool.at[place, z, pl.ds(cut, block_rows - cut)]

    def describe(place, z, part, device, number):
        return pltpu.make_async_remote_copy(
            src_ref=piece(place, z, part), dst_ref=piece(place, z, part),
            send_sem=send_sem.at[number], recv_sem=recv_sem.at[1 if part == 1 else 0, place, z],
            device_id=device, device_id_type=pl.DeviceIdType.MESH,
        )

    def send(place, z, part, device):
        copy = describe(place, z, part, device, len(started))
        copy.start()
        started.append(copy)

    def await_piece(place, z, part=None):
        describe(place, z, part, (region, tile), 0).wait_recv()

    def spread(z):
        for p in x_others + y_others:
            send(at, z, None, (region, at_z * plane + p))

    for z in z_others:
        send(at, at_z, None, (region, z * plane + at))
    spread(at_z)

    for copy in fetched[5:]:
        copy.wait()
    for t in range(tiles):
        near_weights[t] = local_ref[:, t * records:(t + 1) * records]
        lower = edge_ref[:, 2 * t * edges:(2 * t + 1) * edges]
        upper = edge_ref[:, (2 * t + 1) * edges:(2 * t + 2) * edges]
        if sides == 1:
            far_weights[0, t] = jnp.where(region == 0, upper, lower)
        else:
            far_weights[0, t] = lower
            far_weights[1, t] = upper

    def flat(block, count):
        return jnp.concatenate([block[part * count:(part + 1) * count] for part in range(parts)], axis=1)

    def add(data, inverse_var, innovation, loc, first=False):
        scale = loc * inverse_var
        weighted = (scale * innovation).astype(jnp.bfloat16)
        turned = data.astype(jnp.float32).T
        more = jnp.dot(weighted, data, preferred_element_type=jnp.float32)
        innov_ref[...] = more if first else innov_ref[...] + more
        for b in range(boxes):
            scaled = (turned * scale[b:b + 1]).astype(jnp.bfloat16)
            more = jnp.dot(scaled, data, preferred_element_type=jnp.float32)
            gram_ref[b] = more if first else gram_ref[b] + more

    units = []

    def crossing(unit, side):
        extent = pl.ds(0, parts * len(units[unit]) * edges + INFO_ROWS)
        return pltpu.make_async_remote_copy(
            src_ref=leaving.at[side, unit, extent], dst_ref=arriving.at[side, unit, extent],
            send_sem=edge_send_sem.at[side, unit], recv_sem=edge_recv_sem.at[side, unit],
            device_id=(partners[side], tile), device_id_type=pl.DeviceIdType.MESH,
        )

    def near_unit(blocks):
        unit = len(units)
        units.append(blocks)
        data = jnp.concatenate([flat(pool[place, z], records) for place, z in blocks], axis=0)
        infos = [pool[place, z, info_at:, :] for place, z in blocks]
        info = jnp.concatenate(infos, axis=1)
        index_rows = [each.astype(jnp.float32)[2:3] for each in infos]
        picked = len(blocks) * edges
        for side in range(sides):
            if sides == 1:
                index = [jnp.where(region == 0, each[:, :edges], each[:, edges:2 * edges]) for each in index_rows]
                keep = 1.0
            else:
                index = [each[:, side * edges:(side + 1) * edges] for each in index_rows]
                keep = jnp.where(region == (0 if side else regions - 1), 0.0, 1.0)
            index = jnp.concatenate([each + float(n * records) for n, each in enumerate(index)], axis=1)
            index = jnp.concatenate([index, jnp.full((1, LANES - picked), -1.0, jnp.float32)], axis=1) if picked < LANES else index
            row_of = lax.broadcasted_iota(jnp.int32, (len(blocks) * records, LANES), 0).astype(jnp.float32)
            chosen = jnp.where(row_of == index, keep, 0.0)
            far_info = jnp.dot(info, chosen.astype(jnp.bfloat16), preferred_element_type=jnp.float32)
            far = jnp.dot(chosen.T[:picked].astype(jnp.bfloat16), data, preferred_element_type=jnp.float32)
            far = far.astype(jnp.bfloat16)
            for part in range(parts):
                leaving[side, unit, part * picked:(part + 1) * picked, :] = far[:, part * LANES:(part + 1) * LANES]
            leaving[side, unit, parts * picked:parts * picked + INFO_ROWS, :] = far_info.astype(jnp.bfloat16)
            crossing(unit, side).start()
        wide_info = info.astype(jnp.float32)
        loc = jnp.concatenate([near_weights[z * plane + place] for place, z in blocks], axis=1)
        add(data, wide_info[0:1], wide_info[1:2], loc, unit == 0)

    def near_units(blocks):
        for start in range(0, len(blocks), UNIT):
            near_unit(blocks[start:start + UNIT])

    def far_units(first, last):
        data, info, loc = [], [], []
        for unit in range(first, last):
            picked = len(units[unit]) * edges
            for side in range(sides):
                crossing(unit, side).wait_recv()
                data.append(flat(arriving[side, unit, :parts * picked, :], picked))
                info.append(arriving[side, unit, parts * picked:parts * picked + INFO_ROWS, :].astype(jnp.float32)[:, :picked])
                loc += [far_weights[side, z * plane + place] for place, z in units[unit]]
        data = jnp.concatenate(data, axis=0)
        info = jnp.concatenate(info, axis=1)
        add(data, info[0:1], info[1:2], jnp.concatenate(loc, axis=1))

    for z in z_others:
        await_piece(at, z)
        spread(z)
    order = [at_z] + z_others
    near_units([(at, z) for z in order])
    for z in order:
        for p in x_others:
            await_piece(p, z)
            for d in range(1, y_side):
                far = (at_y + d) % y_side * x_side + at_x
                send(p, z, 0, (region, at_z * plane + far))
        for p in y_others:
            await_piece(p, z)
            for d in range(1, x_side):
                far = at_y * x_side + (at_x + d) % x_side
                send(p, z, 1, (region, at_z * plane + far))
        near_units([(p, z) for p in x_others + y_others])
    early = len(units)
    far_units(0, early)
    diagonal = [
        (at_y + dy) % y_side * x_side + (at_x + dx) % x_side
        for dy in range(1, y_side) for dx in range(1, x_side)
    ]
    for start in range(0, z_side, 2):
        blocks = [(far, z) for far in diagonal for z in order[start:start + 2]]
        for far, z in blocks:
            await_piece(far, z, 0)
            await_piece(far, z, 1)
        near_units(blocks)
    far_units(early, len(units))
    for unit in range(len(units)):
        for side in range(sides):
            crossing(unit, side).wait_send()
    for copy in started:
        copy.wait_send()


def gathered_sums(ens_obs, obs_values, obs_var, edge_up, edge_down, loc_local, loc_edge):
    regions, tiles = lax.axis_size("region"), lax.axis_size("tile")
    records, members = ens_obs.shape
    boxes, edges = loc_local.shape[0], edge_up.shape[0]
    sides = 1 if regions == 2 else 2
    z_side, y_side, x_side = tile_sides(tiles)
    plane = y_side * x_side
    block_rows = members // LANES * records + INFO_ROWS
    edge_rows = members // LANES * UNIT * edges + INFO_ROWS
    sideways = x_side + y_side - 2
    corners = (x_side - 1) * (y_side - 1)
    units = 1 + z_side * (-(-sideways // UNIT)) + z_side // 2 * (-(-2 * corners // UNIT))
    sends = z_side - 1 + z_side * (x_side + y_side - 2) + 2 * z_side * (x_side - 1) * (y_side - 1)
    arrays = (ens_obs, obs_values.reshape(1, -1), obs_var.reshape(1, -1), edge_up.reshape(1, -1),
              edge_down.reshape(1, -1), loc_local, loc_edge)
    return pl.pallas_call(
        functools.partial(gather_kernel, regions, tiles),
        out_shape=(
            jax.ShapeDtypeStruct((boxes, members, members), jnp.float32),
            jax.ShapeDtypeStruct((boxes, members), jnp.float32),
        ),
        in_specs=[pl.BlockSpec(memory_space=pl.ANY)] * 7,
        out_specs=[pl.BlockSpec(memory_space=pltpu.VMEM)] * 2,
        scratch_shapes=[pltpu.VMEM(array.shape, array.dtype) for array in arrays] + [
            pltpu.SemaphoreType.DMA((len(arrays),)),
            pltpu.VMEM((plane, z_side, block_rows, LANES), jnp.bfloat16),
            pltpu.VMEM((tiles, boxes, records), jnp.float32),
            pltpu.VMEM((sides, tiles, boxes, edges), jnp.float32),
            pltpu.VMEM((sides, units, edge_rows, LANES), jnp.bfloat16),
            pltpu.VMEM((sides, units, edge_rows, LANES), jnp.bfloat16),
            pltpu.SemaphoreType.DMA((sends,)),
            pltpu.SemaphoreType.DMA((2, plane, z_side)),
            pltpu.SemaphoreType.DMA((sides, units)),
            pltpu.SemaphoreType.DMA((sides, units)),
        ],
        compiler_params=pltpu.CompilerParams(
            collective_id=0, has_side_effects=True, vmem_limit_bytes=56 * 1024 * 1024
        ),
        name="gather_gram",
    )(*arrays)


def split(x):
    high = x.astype(jnp.bfloat16)
    return high, (x - high.astype(jnp.float32)).astype(jnp.bfloat16)


def dot_thrice(left, right):
    left_high, left_low = split(left)
    right_high, right_low = split(right)
    mixed = jnp.dot(left_low, right_high, preferred_element_type=jnp.float32)
    mixed += jnp.dot(left_high, right_low, preferred_element_type=jnp.float32)
    return mixed + jnp.dot(left_high, right_high, preferred_element_type=jnp.float32)


def dot_full(left, right):
    return jnp.dot(left, right, precision=lax.Precision.HIGHEST, preferred_element_type=jnp.float32)


def shrink(error):
    return error * error / (2.0 - error * error)


def analyse_kernel(gram_ref, innov_ref, states_hbm, ids_hbm, out_ref, system_high, system_low, guess, answer,
                   states_ref, ids_ref, copy_sem):
    states_copy = pltpu.make_async_copy(states_hbm, states_ref, copy_sem.at[0])
    ids_copy = pltpu.make_async_copy(ids_hbm, ids_ref, copy_sem.at[1])
    states_copy.start()
    ids_copy.start()
    boxes, members, _ = gram_ref.shape
    fields, cells, _ = states_ref.shape
    rows = lax.broadcasted_iota(jnp.int32, (members, members), 0)
    columns = lax.broadcasted_iota(jnp.int32, (members, members), 1)
    identity = (rows == columns).astype(jnp.float32)
    ridge = members - 1.0

    worst = jnp.float32(0.0)
    errors = []
    for b in range(boxes):
        full = gram_ref[b] + ridge * identity
        top = jnp.maximum(jnp.max(jnp.sum(jnp.abs(full), axis=0, keepdims=True)), ridge)
        first = 2.0 / (top + ridge)
        error = (top - ridge) / (top + ridge)
        mu = 2.0 / (2.0 - error * error)
        high, low = split(full)
        system_high[b] = high
        system_low[b] = low
        start = (mu * first) * (2.0 * identity - first * full)
        guess[b] = start.astype(jnp.bfloat16)
        answer[b] = start
        errors.append(shrink(error))
        worst = jnp.maximum(worst, top / ridge)

    def coarse(carried):
        after = []
        for b in range(boxes):
            error = carried[b]
            mu = 2.0 / (2.0 - error * error)
            held = guess[b]
            left = identity - jnp.dot(system_high[b], held, preferred_element_type=jnp.float32)
            more = jnp.dot(held, left.astype(jnp.bfloat16), preferred_element_type=jnp.float32)
            guess[b] = (mu * (held.astype(jnp.float32) + more)).astype(jnp.bfloat16)
            after.append(shrink(error))
        return tuple(after)

    def refine(dot):
        def step(carried):
            after = []
            for b in range(boxes):
                error = carried[b]
                mu = 2.0 / (2.0 - error * error)
                full = gram_ref[b] + ridge * identity
                left = 2.0 * identity - dot(full, answer[b])
                answer[b] = mu * dot(answer[b], left)
                after.append(shrink(error))
            return tuple(after)
        return step

    def above(limit):
        def proceed(carried):
            top = carried[0]
            for error in carried[1:]:
                top = jnp.maximum(top, error)
            return top > limit
        return proceed

    easy = worst < 64.0
    hard = worst > 2048.0

    @pl.when(easy)
    def _():
        lax.while_loop(above(0.02), coarse, tuple(errors))
        for b in range(boxes):
            held = guess[b]
            left = identity - jnp.dot(system_high[b], held, preferred_element_type=jnp.float32)
            left = left - jnp.dot(system_low[b], held, preferred_element_type=jnp.float32)
            more = jnp.dot(held, left.astype(jnp.bfloat16), preferred_element_type=jnp.float32)
            answer[b] = held.astype(jnp.float32) + more

    @pl.when(jnp.logical_and(jnp.logical_not(easy), jnp.logical_not(hard)))
    def _():
        lax.while_loop(above(3e-4), refine(dot_thrice), tuple(errors))

    @pl.when(hard)
    def _():
        lax.while_loop(above(1e-6), refine(dot_full), tuple(errors))

    states_copy.wait()
    ids_copy.wait()
    wide = states_ref[...].astype(jnp.float32).reshape(fields * cells, members)
    smean = jnp.sum(wide, axis=1, keepdims=True) * (1.0 / members)
    anomaly = (wide - smean).astype(jnp.bfloat16)
    here = lax.broadcasted_iota(jnp.int32, (cells, cells), 0) == lax.broadcasted_iota(jnp.int32, (cells, cells), 1)
    spread = jnp.broadcast_to(ids_ref[...].astype(jnp.float32), (cells, cells))
    ids = jnp.sum(jnp.where(here, spread, 0.0), axis=1, keepdims=True)
    ids = jnp.concatenate([ids] * fields, axis=0)
    total = jnp.zeros((fields * cells, members), jnp.float32)
    for b in range(boxes):
        inverse = answer[b]
        wbar = jnp.sum(inverse * innov_ref[b:b + 1, :], axis=1, keepdims=True)
        transform = (0.5 * identity + (0.5 * ridge) * inverse + wbar).astype(jnp.bfloat16)
        update = jnp.dot(anomaly, transform, preferred_element_type=jnp.float32)
        total = jnp.where(ids == float(b), update, total)
    out_ref[...] = (smean + total).astype(jnp.bfloat16).reshape(fields, cells, members)


def analyse(gram, innov, states, box_ids):
    boxes, members, _ = gram.shape
    square = (boxes, members, members)
    return pl.pallas_call(
        analyse_kernel,
        out_shape=jax.ShapeDtypeStruct(states.shape, jnp.bfloat16),
        in_specs=[pl.BlockSpec(memory_space=pltpu.VMEM)] * 2 + [pl.BlockSpec(memory_space=pl.ANY)] * 2,
        out_specs=pl.BlockSpec(memory_space=pltpu.VMEM),
        scratch_shapes=[
            pltpu.VMEM(square, jnp.bfloat16),
            pltpu.VMEM(square, jnp.bfloat16),
            pltpu.VMEM(square, jnp.bfloat16),
            pltpu.VMEM(square, jnp.float32),
            pltpu.VMEM(states.shape, jnp.bfloat16),
            pltpu.VMEM((1, box_ids.shape[0]), jnp.int32),
            pltpu.SemaphoreType.DMA((2,)),
        ],
        compiler_params=pltpu.CompilerParams(vmem_limit_bytes=56 * 1024 * 1024),
        name="analyse",
    )(gram, innov, states, box_ids.reshape(1, -1))


def body(ens_obs, obs_values, obs_var, edge_up, edge_down, loc_local, loc_edge, states, box_ids):
    gram, innov = gathered_sums(ens_obs, obs_values, obs_var, edge_up, edge_down, loc_local, loc_edge)
    return analyse(gram, innov, states, box_ids)


def solution(mesh):
    return jax.shard_map(
        body,
        mesh=mesh,
        in_specs=(
            P(("region", "tile"), None),
            P(("region", "tile")),
            P(("region", "tile")),
            P(("region", "tile")),
            P(("region", "tile")),
            P(("region", "tile"), None),
            P(("region", "tile"), None),
            P(None, ("region", "tile"), None),
            P(("region", "tile")),
        ),
        out_specs=P(None, ("region", "tile"), None),
        check_vma=False,
    )
```
